32 devices in a mesh: members: 2 (over x), tile: 8 (over z, y), sub: 2 (over core).
Axes of the slice: x: 2, y: 2, z: 4, core: 2. Of those that a mesh axis runs over, the one named last changes fastest.
Arguments:
- tracers: float32 [40, 12, 32768], P('members', None, ('tile', 'sub')), parts along dimension 0, may hold values from -6 to 6
- courant: float32 [40, 32768], P('members', ('tile', 'sub')), parts along dimension 0, may hold values from 0.1 to 0.9
- air_surface: float32 [8, 32768], P('members', ('tile', 'sub')), parts along dimension 0, may hold values from -6 to 6
- block_weights: bfloat16 [4096, 128, 128], P(('tile', 'sub')), may hold values from 0 to 0.015625
- block_dest: int32 [4096, 1], replicated, may hold values from 0 to 15; in each aligned block of 256 rows (0 to 255, 256 to 511, ...) at most 32 rows name the same one
- block_row: int32 [4096], replicated, may hold values from 0 to 15
- block_patch: int32 [4096], P(('tile', 'sub')), may hold values from 0 to 15
- ocean_state: float32 [32, 32, 1024], P('members', 'sub', 'tile'), parts along dimension 0, may hold values from -6 to 6
- exchange_rate: float32 [32, 1024], P('sub', 'tile'), may hold values from 0.05 to 0.5
- sea_mask: int32 [32, 1024], P('sub', 'tile'), may hold values 0 or 1
Outputs:
- tracers_out: float32 [40, 12, 32768], P('members', None, ('tile', 'sub')), parts along dimension 0
- ocean_next: float32 [32, 32, 1024], P('members', 'sub', 'tile'), parts along dimension 0
- air_exchange: float32 [32, 32768], P('members', ('tile', 'sub')), parts along dimension 0
The draws below stay inside these ranges and needn't reach their ends.
There are 2 independent parts, one for each index of `members`. The reference program is written for one: setup_inputs(seed, part) draws one part's arguments, and reference() takes and returns one part's arrays. A program takes and returns all parts, laid end to end along the dimension named above; an argument that names none is the same for every part. Nothing has to cross between parts.
Inputs may be any that keep to these rules, and one draw needn't show every extreme that they name: `block_dest`: in the 256 rows of one device no ocean device is named more than 32 times, a bound that some block reaches.
All inputs are finite; a program needn't handle non-finite values. No bound on the sum of `sea_mask` on one device may be relied on, other than what follows from the above.
Results may differ from the reference program's by a relative error of at most 0.0026.
Values may be sent and summed in bfloat16 or wider, within the bound.
No kernel may reach another device: no remote copies, remote signals or barrier semaphores. Data moves between devices by JAX's collectives and lax.ppermute only.
A program may use at most 128 MiB of HBM per device.

```python
import math
import jax
import jax.numpy as jnp
import numpy as np
from jax import lax

Q = 12
AIRF = 4
NF = 16
L = 20
ASTEPS = 3
PATCH = 128
APD = 16
OY = 16
KB = 256
DEVS = 16
CAP = 32
NA_TOTAL = 32768
NBLK = 4096
NXO = 1024
NYO = 32
N_TILE = 8
N_SUB = 2


def with_ends(result, own_key, least, high):
    shape = result.shape
    place = [jax.random.randint(jax.random.fold_in(own_key, axis), (), 0, shape[axis]) for axis in range(len(shape))]
    result = result.at[tuple(place)].set(least)
    longest = shape.index(max(shape))
    place[longest] = (place[longest] + 1) % shape[longest]
    return result.at[tuple(place)].set(high)


def block_levels(stream_key, extent, cuts, smallest, top_value):
    gain = 1.0
    for dim, shards_of in cuts:
        heights = jax.random.uniform(jax.random.fold_in(jax.random.fold_in(stream_key, 6), dim), (shards_of,), jnp.float32, smallest / len(cuts), top_value / len(cuts))
        gain = gain * jnp.repeat(jnp.exp(heights), extent[dim] // shards_of).reshape((-1,) + (1,) * (len(extent) - 1 - dim))
    return gain


def shared_out(rng, own, number, rows, count, top, most, slope):
    ranking = jax.random.permutation(rng, count)
    packed, usual = load_shares(count, rows * top, most, slope, True), load_shares(count, rows * top, most, slope, False)
    places = jnp.arange(count)

    def named(tallies, offset_by):
        used = int((tallies > 0).sum())
        fixed = max(1, used // 4)
        moved = fixed + (places - fixed + offset_by * (used - fixed)) % max(1, count - fixed)
        return jnp.zeros((count,), jnp.int32).at[ranking[jnp.where(places < fixed, places, moved)]].set(jnp.asarray(tallies, jnp.int32))

    tallies = jnp.where(number % 4 == 0, named(packed, number // 4), named(usual, number - number // 4 - 1))
    mixed = jax.random.permutation(jax.random.fold_in(own, 3), count)
    giver, taker = mixed[0:count // 2 * 2:2], mixed[1:count // 2 * 2:2]
    margin = jnp.minimum(tallies[giver] - 1, most - tallies[taker]) // 2
    margin = jnp.where((giver == ranking[0]) | (taker == ranking[0]) | (tallies[taker] == 0), 0, jnp.maximum(margin, 0))
    moved = jax.random.randint(jax.random.fold_in(own, 4), (count // 2,), 0, 1 << 20) % (margin + 1)
    tallies = tallies.at[giver].add(-moved).at[taker].add(moved)
    items = jnp.searchsorted(jnp.cumsum(tallies), jnp.arange(rows * top), side="right").astype(jnp.int32)
    grid = items.reshape(top, rows).T
    grid = grid[jax.random.permutation(jax.random.fold_in(own, 1), rows)]
    offset_by = jax.random.randint(jax.random.fold_in(own, 2), (rows, 1), 0, top)
    return jnp.take_along_axis(grid, (jnp.arange(top)[None, :] + offset_by) % top, axis=1)


def load_shares(count, total, most, skew, full):
    loads = [(1 << 20) // math.isqrt(standing ** skew) + 1 for standing in range(1, count + 1)]
    largest = most if full else min(most, max(-(-total // count), total * loads[0] // sum(loads)))
    least = 1 if total - largest >= count - 1 else 0
    counts, rest = [largest] + [least] * (count - 1), total - largest - least * (count - 1)
    while rest > 0:
        candidates = [i for i in range(1, count) if counts[i] < largest] or [i for i in range(1, count) if counts[i] < most]
        mass, remaining = sum([loads[i] for i in candidates]), rest
        for i in candidates:
            addition = min(most - counts[i], max(1, remaining * loads[i] // mass), rest)
            counts[i] = counts[i] + addition
            rest = rest - addition
    return np.array(counts)


def noise(own_key, extent, deviation, bound, shards=(), held_as=jnp.bfloat16):
    gain = block_levels(own_key, extent, shards, -0.22, 0.18) if shards else 1.0
    result = jax.random.normal(own_key, extent, jnp.float32) * deviation * gain
    return jnp.minimum(jnp.maximum(result, -bound), bound).astype(held_as)


def setup_inputs(seed: int = 0, part: int = 0) -> dict:
    key_of = jax.random.split(jax.random.key(seed), 11)
    part_keys = jax.random.split(jax.random.fold_in(key_of[10], part), 11)
    tracers = noise(part_keys[0], (L, Q, NA_TOTAL), 1.0, 6.0, ((2, 16),), jnp.float32)
    courant = jnp.clip(0.1 + 0.79999997 * jax.random.uniform(part_keys[1], (L, NA_TOTAL), jnp.float32) ** block_levels(part_keys[1], (L, NA_TOTAL), ((1, 16),), -0.2, 0.2), 0.1, 0.9)
    air_surface = noise(part_keys[2], (AIRF, NA_TOTAL), 1.0, 6.0, ((1, 16),), jnp.float32)
    block_weights = jnp.clip(0.015625 * jax.random.uniform(key_of[3], (NBLK, PATCH, PATCH), jnp.float32) ** block_levels(key_of[3], (NBLK, PATCH, PATCH), ((0, 16),), -0.2, 0.2), 0.0, 0.015625).astype(jnp.bfloat16)
    block_dest_keys = jax.random.split(jax.random.fold_in(key_of[4], 1), NBLK // KB)
    block_dest_turns = jax.random.permutation(jax.random.fold_in(key_of[4], 3), NBLK // KB)
    block_dest = jax.vmap(lambda own, number: shared_out(jax.random.fold_in(key_of[4], 2), own, number, KB, DEVS, 1, CAP, 2))(block_dest_keys, block_dest_turns).reshape((NBLK, 1))
    block_row = with_ends(jax.random.randint(key_of[5], (NBLK,), 0, OY), jax.random.fold_in(key_of[5], 1), 0, OY - 1).astype(jnp.int32)
    block_patch = with_ends(jax.random.randint(key_of[6], (NBLK,), 0, APD), jax.random.fold_in(key_of[6], 1), 0, APD - 1).astype(jnp.int32)
    ocean_state = noise(part_keys[7], (NF, NYO, NXO), 1.0, 6.0, ((1, 2), (2, 8)), jnp.float32)
    exchange_rate = jnp.clip(jnp.exp(math.log(0.5) - 2.3025851 * jax.random.uniform(key_of[8], (NYO, NXO), jnp.float32) ** block_levels(key_of[8], (NYO, NXO), ((0, 2), (1, 8)), -0.2, 0.2)), 0.05, 0.5)
    sea_mask = with_ends((jax.random.randint(key_of[9], (NYO, NXO), 0, 4) < 3).astype(jnp.int32), jax.random.fold_in(key_of[9], 1), 0, 1)
    return dict(tracers=tracers, courant=courant, air_surface=air_surface, block_weights=block_weights, block_dest=block_dest, block_row=block_row, block_patch=block_patch, ocean_state=ocean_state, exchange_rate=exchange_rate, sea_mask=sea_mask)


NU = 0.2
COUPLE = 0.5


def ppm_step(padded, courant_pad, span_cells):
    edge_vals = (7.0 * (padded[..., 1:span_cells + 3] + padded[..., 2:span_cells + 4])
                 - (padded[..., 0:span_cells + 2] + padded[..., 3:span_cells + 5])) / 12.0
    left_edge = edge_vals[..., 0:span_cells + 1]
    right_edge = edge_vals[..., 1:span_cells + 2]
    centre = padded[..., 2:span_cells + 3]
    number = courant_pad[:, None, 2:span_cells + 3]
    curvature = 6.0 * (centre - 0.5 * (left_edge + right_edge))
    fluxes = number * (right_edge - 0.5 * number * (right_edge - left_edge - (1.0 - 2.0 * number / 3.0) * curvature))
    return padded[..., 3:span_cells + 3] - (fluxes[..., 1:] - fluxes[..., :-1])


def periodic(values):
    return jnp.concatenate([values[..., -3:], values, values[..., :3]], axis=-1)


def forward_group(operands):
    return jnp.einsum("bfi,bij->bfj", operands[0].astype(jnp.float32), operands[1].astype(jnp.float32))


def backward_group(operands):
    return jnp.einsum("bfj,bij->bfi", operands[0].astype(jnp.float32), operands[1].astype(jnp.float32))


def reference(tracers, courant, air_surface, block_weights, block_dest, block_row, block_patch, ocean_state, exchange_rate, sea_mask):
    courant_pad = periodic(courant)
    advected = tracers
    for substep in range(ASTEPS):
        advected = ppm_step(periodic(advected), courant_pad, NA_TOTAL)
    surface = jnp.concatenate([advected[0], air_surface], axis=0).astype(jnp.bfloat16)
    patch_rows = surface.reshape(NF, DEVS * APD, PATCH).transpose(1, 0, 2)
    source_dev = jnp.arange(NBLK, dtype=jnp.int32) // KB
    patch_global = (source_dev * APD + block_patch).astype(jnp.int32)
    dest_dev = block_dest[:, 0]
    ocean_index = (((dest_dev % N_SUB) * OY + block_row) * N_TILE + dest_dev // N_SUB).astype(jnp.int32)
    weight_groups = block_weights.reshape(DEVS, KB, PATCH, PATCH)
    gathered = patch_rows[patch_global].reshape(DEVS, KB, NF, PATCH)
    pieces = lax.map(forward_group, (gathered, weight_groups)).reshape(NBLK, NF, PATCH)
    received = jax.ops.segment_sum(pieces, ocean_index, num_segments=NYO * N_TILE)
    remapped = received.reshape(NYO, N_TILE, NF, PATCH).transpose(2, 0, 1, 3).reshape(NF, NYO, NXO)
    fold_sign = jnp.where(jnp.arange(NF) >= NF - 2, -1.0, 1.0).astype(jnp.float32)
    fold_row = fold_sign[:, None] * ocean_state[:, -1, ::-1]
    below_rows = jnp.concatenate([jnp.zeros_like(ocean_state[:, :1]), ocean_state[:, :-1]], axis=1)
    above_rows = jnp.concatenate([ocean_state[:, 1:], fold_row[:, None]], axis=1)
    lateral = jnp.roll(ocean_state, 1, 2) + jnp.roll(ocean_state, -1, 2) + below_rows + above_rows - 4.0 * ocean_state
    wet_cells = sea_mask.astype(jnp.float32)
    ocean_next = ocean_state + wet_cells * (exchange_rate * (remapped - ocean_state) + NU * lateral)
    ocean_rows = ocean_next.astype(jnp.bfloat16).reshape(NF, NYO, N_TILE, PATCH).transpose(1, 2, 0, 3).reshape(NYO * N_TILE, NF, PATCH)
    returned = ocean_rows[ocean_index].reshape(DEVS, KB, NF, PATCH)
    spread = lax.map(backward_group, (returned, weight_groups)).reshape(NBLK, NF, PATCH)
    collected = jax.ops.segment_sum(spread, patch_global, num_segments=DEVS * APD)
    air_exchange = collected.transpose(1, 0, 2).reshape(NF, NA_TOTAL)
    tracers_out = advected.at[0].add(COUPLE * air_exchange[:Q])
    return tracers_out, ocean_next, air_exchange
```

```python
import functools

import jax
import jax.numpy as jnp
from jax import lax
from jax.experimental import pallas as pl
from jax.experimental.pallas import tpu as pltpu
from jax.sharding import PartitionSpec as P

ASTEPS = 3
NU = 0.2
COUPLE = 0.5
LANES = 128
EDGE = 16
GROUPS = LANES // EDGE
UNROLL = 16
BIG = 48 * 1024 * 1024

VMEM = pl.BlockSpec(memory_space=pltpu.VMEM)
SMEM = pl.BlockSpec(memory_space=pltpu.SMEM)
ANY = pl.BlockSpec(memory_space=pl.ANY)
f32 = jnp.float32
bf16 = jnp.bfloat16


def params(limit=BIG):
    return pltpu.CompilerParams(vmem_limit_bytes=limit)


def lane_roll(x, shift):
    length = x.shape[-1]
    shift = shift % length
    return x if shift == 0 else pltpu.roll(x, shift, x.ndim - 1)


def coefficients(c):
    d = 1.0 - c
    return c * d * d * (1.0 / 12.0), c * c * d * (1.0 / 12.0), c * c * (3.0 - 2.0 * c)


def advect(q, right, left, own):
    for _ in range(ASTEPS):
        pair = q + lane_roll(q, -1)
        edge = 8.0 * pair - (lane_roll(pair, 1) + lane_roll(pair, -1))
        flux = right * edge - left * lane_roll(edge, 1) + own * q
        q = q - (flux - lane_roll(flux, 1))
    return q


def pack_kernel(tracers, levels, parity_ref, left_t, right_t, left_c, right_c, a_ref, b_ref):
    parity = parity_ref[0]
    lane = lax.broadcasted_iota(jnp.int32, (levels, LANES), 1)
    pad = pl.cdiv(levels, 8) * 8
    for out, from_left in ((a_ref, parity == 1), (b_ref, parity == 0)):
        for part in range(pl.cdiv(tracers + 1, GROUPS)):
            total = jnp.zeros((levels, LANES), f32)
            for group in range(GROUPS):
                item = part * GROUPS + group
                if item > tracers:
                    continue
                low = left_t[item] if item < tracers else left_c[...]
                high = right_t[item] if item < tracers else right_c[...]
                moved = jnp.where(
                    from_left,
                    lane_roll(low, EDGE * group),
                    lane_roll(high, EDGE * (group + 1)),
                )
                total = jnp.where(lane // EDGE == group, moved, total)
            out[part * pad : part * pad + levels, :] = total
        top = pl.cdiv(tracers + 1, GROUPS) * pad
        for item in range(tracers):
            out[top + item : top + item + 1, :] = jnp.where(
                from_left, left_t[item, 0:1, :], right_t[item, 0:1, :]
            )
        out[top + tracers : top + tracers + 1, :] = jnp.where(
            from_left, left_c[0:1, :], right_c[0:1, :]
        )


def pack(tracers_t, courant, parity):
    tracers, levels, span = tracers_t.shape
    last = span // LANES - 1
    pad = pl.cdiv(levels, 8) * 8
    rows = pl.cdiv(tracers + 1, GROUPS) * pad + pl.cdiv(tracers + 1, 8) * 8
    message = jax.ShapeDtypeStruct((rows, LANES), f32)
    return pl.pallas_call(
        functools.partial(pack_kernel, tracers, levels),
        grid=(1,),
        out_shape=(message, message),
        in_specs=[
            SMEM,
            pl.BlockSpec((tracers, levels, LANES), lambda i: (0, 0, 0)),
            pl.BlockSpec((tracers, levels, LANES), lambda i: (0, 0, last)),
            pl.BlockSpec((levels, LANES), lambda i: (0, 0)),
            pl.BlockSpec((levels, LANES), lambda i: (0, last)),
        ],
        out_specs=(
            pl.BlockSpec((rows, LANES), lambda i: (0, 0)),
            pl.BlockSpec((rows, LANES), lambda i: (0, 0)),
        ),
        compiler_params=params(16 * 1024 * 1024),
        name="pack_edges",
    )(parity, tracers_t, tracers_t, courant, courant)


def forward_kernel(
    dims,
    parity_ref,
    slot_ref,
    patch_ref,
    level0,
    courant0,
    air,
    msg_a,
    msg_b,
    weights_hbm,
    send_ref,
    keep_ref,
    weights,
    surface,
    total,
    sems,
):
    tracers, span, top, pieces_n, per_piece = dims
    copies = [
        pltpu.make_async_copy(
            weights_hbm.at[pl.ds(i * per_piece, per_piece)],
            weights.at[pl.ds(i * per_piece, per_piece)],
            sems.at[i],
        )
        for i in range(pieces_n)
    ]
    for copy in copies:
        copy.start()
    even = parity_ref[0] == 0
    a, b = msg_a[top : top + tracers + 1, :], msg_b[top : top + tracers + 1, :]
    left, right = jnp.where(even, b, a), jnp.where(even, a, b)
    q = jnp.concatenate([left[:tracers], level0[...], right[:tracers]], axis=1)
    c = jnp.concatenate([left[tracers:], courant0[0:1, :], right[tracers:]], axis=1)
    advected = advect(q, *coefficients(c))[:, LANES : LANES + span]
    fields = jnp.concatenate([advected, air[...]], axis=0).astype(bf16)
    for p in range(span // LANES):
        surface[p] = fields[:, p * LANES : (p + 1) * LANES]
    total[...] = jnp.zeros_like(total)

    for i in range(pieces_n):
        copies[i].wait()

        def step(g, carry, i=i):
            base = i * per_piece + g * UNROLL
            products = []
            for u in range(UNROLL):
                products.append(
                    jnp.dot(
                        surface[patch_ref[base + u]],
                        weights[base + u],
                        preferred_element_type=f32,
                    )
                )
            for u in range(UNROLL):
                total[slot_ref[base + u]] += products[u]
            return carry

        lax.fori_loop(0, per_piece // UNROLL, step, 0)
    half = total.shape[0] // 2
    keep_ref[...] = total[:half]
    send_ref[...] = total[half:].astype(bf16)


def forward(parity, slot, patch, level0, courant, air, msg_a, msg_b, weights, rows):
    tracers, span = level0.shape
    levels = courant.shape[0]
    blocks = weights.shape[0]
    fields = tracers + air.shape[0]
    pieces_n = 8
    pad = pl.cdiv(levels, 8) * 8
    top = pl.cdiv(tracers + 1, GROUPS) * pad
    dims = (tracers, span, top, pieces_n, blocks // pieces_n)
    return pl.pallas_call(
        functools.partial(forward_kernel, dims),
        out_shape=(
            jax.ShapeDtypeStruct((rows // 2, fields, LANES), bf16),
            jax.ShapeDtypeStruct((rows // 2, fields, LANES), f32),
        ),
        in_specs=[SMEM, SMEM, SMEM, VMEM, VMEM, VMEM, VMEM, VMEM, ANY],
        out_specs=(VMEM, VMEM),
        scratch_shapes=[
            pltpu.VMEM(weights.shape, bf16),
            pltpu.VMEM((span // LANES, fields, LANES), bf16),
            pltpu.VMEM((rows, fields, LANES), f32),
            pltpu.SemaphoreType.DMA((pieces_n,)),
        ],
        compiler_params=params(),
        name="blocks_to_rows",
    )(parity, slot, patch, level0, courant, air, msg_a, msg_b, weights)


def merge_kernel(chunk, keep, got, own_ref, *outs):
    own_ref[...] = keep[:chunk] + got[:chunk].astype(f32)
    for d, out in enumerate(outs):
        part = slice((d + 1) * chunk, (d + 2) * chunk)
        out[...] = (keep[part] + got[part].astype(f32)).astype(bf16)


def merge(keep, got, chunk):
    rows, fields, lanes = keep.shape
    count = rows // chunk
    return pl.pallas_call(
        functools.partial(merge_kernel, chunk),
        out_shape=(jax.ShapeDtypeStruct((chunk, fields, lanes), f32),)
        + (jax.ShapeDtypeStruct((chunk, fields, lanes), bf16),) * (count - 1),
        in_specs=[VMEM, VMEM],
        out_specs=(VMEM,) * count,
        compiler_params=params(),
        name="merge_cores",
    )(keep, got)


def ocean_kernel(
    count, state, south, north, east_west, rate, wet, own, *rest
):
    got, (next_ref, half_ref) = rest[:count], rest[count:]
    rows, fields, lanes = state.shape
    lane = lax.broadcasted_iota(jnp.int32, (fields, lanes), 1)
    from_west, from_east = east_west[0], east_west[1]
    for r in range(rows):
        here = state[r]
        west = jnp.where(lane == 0, lane_roll(from_west, -r), lane_roll(here, 1))
        east = jnp.where(
            lane == lanes - 1, lane_roll(from_east, lanes - 1 - rows - r), lane_roll(here, -1)
        )
        below = state[r - 1] if r else south[...]
        above = state[r + 1] if r < rows - 1 else north[...]
        lateral = west + east + below + above - 4.0 * here
        remapped = own[r]
        for chunk in got:
            remapped = remapped + chunk[r].astype(f32)
        new = here + wet[r : r + 1, :].astype(f32) * (
            rate[r : r + 1, :] * (remapped - here) + NU * lateral
        )
        next_ref[r] = new
        half_ref[r] = new.astype(bf16)


def ocean(state, south, north, east_west, rate, wet, own, got):
    return pl.pallas_call(
        functools.partial(ocean_kernel, len(got)),
        out_shape=(
            jax.ShapeDtypeStruct(state.shape, f32),
            jax.ShapeDtypeStruct(state.shape, bf16),
        ),
        in_specs=[VMEM] * (7 + len(got)),
        out_specs=(VMEM, VMEM),
        compiler_params=params(),
        name="ocean_update",
    )(state, south, north, east_west, rate, wet, own, *got)


def edges_kernel(state, out_ref):
    rows, fields, lanes = state.shape
    lane = lax.broadcasted_iota(jnp.int32, (fields, lanes), 1)
    total = jnp.zeros((fields, lanes), f32)
    for r in range(rows):
        total = jnp.where(lane == r, lane_roll(state[r], r + 1), total)
        total = jnp.where(lane == rows + r, lane_roll(state[r], rows + r), total)
    out_ref[...] = total


def ocean_edges(state):
    rows, fields, lanes = state.shape
    return pl.pallas_call(
        edges_kernel,
        out_shape=jax.ShapeDtypeStruct((fields, lanes), f32),
        in_specs=[VMEM],
        out_specs=VMEM,
        compiler_params=params(16 * 1024 * 1024),
        name="ocean_edges",
    )(state)


def advect_kernel(tracers, levels, parity_ref, q_ref, c_ref, msg_a, msg_b, out_ref, right, left, own):
    item = pl.program_id(0)
    even = parity_ref[0] == 0
    span = q_ref.shape[2]
    pad = pl.cdiv(levels, 8) * 8

    def sides(part, group):
        start = pl.multiple_of(part * pad, 8)
        a, b = msg_a[pl.ds(start, levels), :], msg_b[pl.ds(start, levels), :]
        low, high = jnp.where(even, b, a), jnp.where(even, a, b)
        shift = EDGE * group
        return (
            pltpu.roll(low, (2 * LANES - EDGE - shift) % LANES, 1),
            pltpu.roll(high, (LANES - shift) % LANES, 1),
        )

    @pl.when(item == 0)
    def _():
        low, high = sides(tracers // GROUPS, tracers % GROUPS)
        c = jnp.concatenate([low, c_ref[...], high], axis=1)
        right[...], left[...], own[...] = coefficients(c)

    low, high = sides(item // GROUPS, item % GROUPS)
    q = jnp.concatenate([low, q_ref[0], high], axis=1)
    out_ref[0] = advect(q, right[...], left[...], own[...])[:, LANES : LANES + span]


def advect_all(parity, tracers_t, courant, msg_a, msg_b):
    tracers, levels, span = tracers_t.shape
    wide = span + 2 * LANES
    whole = lambda shape: pl.BlockSpec(shape, lambda i: (0,) * len(shape))
    return pl.pallas_call(
        functools.partial(advect_kernel, tracers, levels),
        grid=(tracers,),
        out_shape=jax.ShapeDtypeStruct(tracers_t.shape, f32),
        in_specs=[
            SMEM,
            pl.BlockSpec((1, levels, span), lambda i: (i, 0, 0)),
            whole(courant.shape),
            whole(msg_a.shape),
            whole(msg_b.shape),
        ],
        out_specs=pl.BlockSpec((1, levels, span), lambda i: (i, 0, 0)),
        scratch_shapes=[pltpu.VMEM((levels, wide), f32)] * 3,
        compiler_params=params(16 * 1024 * 1024),
        cost_estimate=pl.CostEstimate(
            flops=60 * tracers * levels * span,
            bytes_accessed=8 * tracers * levels * span,
            transcendentals=0,
        ),
        name="advect_levels",
    )(parity, tracers_t, courant, msg_a, msg_b)


def backward_kernel(
    dims,
    slot_ref,
    patch_ref,
    mine,
    other,
    weights_hbm,
    advected_hbm,
    air_ref,
    out_hbm,
    weights,
    rows,
    total,
    bottom,
    sems,
    bottom_sem,
):
    tracers, span, pieces_n, per_piece = dims
    copies = [
        pltpu.make_async_copy(
            weights_hbm.at[pl.ds(i * per_piece, per_piece)],
            weights.at[pl.ds(i * per_piece, per_piece)],
            sems.at[i],
        )
        for i in range(pieces_n)
    ]
    for copy in copies:
        copy.start()
    fetch = pltpu.make_async_copy(advected_hbm.at[:, pl.ds(0, 8), :], bottom, bottom_sem)
    fetch.start()
    half = mine.shape[0]
    rows[:half] = mine[...]
    rows[half:] = other[...]
    total[...] = jnp.zeros_like(total)

    for i in range(pieces_n):
        copies[i].wait()

        def step(g, carry, i=i):
            base = i * per_piece + g * UNROLL
            products = []
            for u in range(UNROLL):
                products.append(
                    lax.dot_general(
                        rows[slot_ref[base + u]],
                        weights[base + u],
                        (((1,), (1,)), ((), ())),
                        preferred_element_type=f32,
                    )
                )
            for u in range(UNROLL):
                total[patch_ref[base + u]] += products[u]
            return carry

        lax.fori_loop(0, per_piece // UNROLL, step, 0)
    fetch.wait()
    for p in range(span // LANES):
        part = slice(p * LANES, (p + 1) * LANES)
        exchange = total[p]
        air_ref[:, part] = exchange
        bottom[:, 0, part] += COUPLE * exchange[:tracers]
    store = pltpu.make_async_copy(bottom, out_hbm.at[:, pl.ds(0, 8), :], bottom_sem)
    store.start()
    store.wait()


def backward(slot, patch, mine, other, weights, advected):
    tracers, levels, span = advected.shape
    blocks = weights.shape[0]
    half, fields, lanes = mine.shape
    pieces_n = 8
    dims = (tracers, span, pieces_n, blocks // pieces_n)
    return pl.pallas_call(
        functools.partial(backward_kernel, dims),
        out_shape=(
            jax.ShapeDtypeStruct((fields, span), f32),
            jax.ShapeDtypeStruct(advected.shape, f32),
        ),
        in_specs=[SMEM, SMEM, VMEM, VMEM, ANY, ANY],
        out_specs=(VMEM, ANY),
        input_output_aliases={5: 1},
        scratch_shapes=[
            pltpu.VMEM(weights.shape, bf16),
            pltpu.VMEM((2 * half, fields, lanes), bf16),
            pltpu.VMEM((span // lanes, fields, lanes), f32),
            pltpu.VMEM((tracers, 8, span), f32),
            pltpu.SemaphoreType.DMA((pieces_n,)),
            pltpu.SemaphoreType.DMA,
        ],
        compiler_params=params(),
        name="rows_to_columns",
    )(slot, patch, mine, other, weights, advected)


def per_device(
    tracers,
    courant,
    air_surface,
    block_weights,
    block_dest,
    block_row,
    block_patch,
    ocean_state,
    exchange_rate,
    sea_mask,
):
    tiles, subs = lax.axis_size("tile"), lax.axis_size("sub")
    devices = tiles * subs
    my_tile, my_sub = lax.axis_index("tile"), lax.axis_index("sub")
    my_index = my_tile * subs + my_sub
    blocks = block_weights.shape[0]
    fields, ocean_rows, lanes = ocean_state.shape
    flat = ("tile", "sub")
    parity = (my_index % 2).astype(jnp.int32).reshape(1)

    tracers_t = jnp.transpose(tracers, (1, 0, 2))
    pack_a, pack_b = pack(tracers_t, courant, parity)
    msg_a = lax.ppermute(pack_a, flat, [(i, i ^ 1) for i in range(devices)])
    msg_b = lax.ppermute(
        pack_b, flat, [(i, (i + 1 if i % 2 else i - 1) % devices) for i in range(devices)]
    )

    start = my_index * blocks
    dest = lax.dynamic_slice(block_dest.reshape(-1), (start,), (blocks,))
    row = lax.dynamic_slice(block_row, (start,), (blocks,))
    chunk_of = ((dest // subs) ^ my_tile) + tiles * ((dest % subs + subs - my_sub) % subs)
    slot = chunk_of * ocean_rows + row

    keep_send = forward(
        parity, slot, block_patch, tracers[0], courant, air_surface, msg_a, msg_b,
        block_weights, devices * ocean_rows,
    )
    send, keep = keep_send
    swap = [(0, 1), (1, 0)]
    own, *partial = merge(keep, lax.ppermute(send, "sub", swap), ocean_rows)
    across = lambda x, d: lax.ppermute(x, "tile", [(i, i ^ d) for i in range(tiles)])
    got = [across(x, d) for d, x in reversed(list(enumerate(partial, 1)))]

    advected = advect_all(parity, tracers_t, courant, msg_a, msg_b)

    state = jnp.transpose(ocean_state, (1, 0, 2))
    edges = ocean_edges(state)
    east_west = jnp.stack(
        [
            lax.ppermute(edges, "tile", [(i, (i + 1) % tiles) for i in range(tiles)]),
            lax.ppermute(edges, "tile", [((i + 1) % tiles, i) for i in range(tiles)]),
        ]
    )
    sign = jnp.where(jnp.arange(fields) >= fields - 2, -1.0, 1.0).astype(f32)[:, None]
    fold = lax.ppermute(
        sign * state[-1][:, ::-1], "tile", [(i, tiles - 1 - i) for i in range(tiles)]
    )
    is_top = my_sub == subs - 1
    beside = lax.ppermute(jnp.where(is_top, state[0], state[-1]), "sub", swap)
    south = jnp.where(my_sub == 0, 0.0, beside)
    north = jnp.where(is_top, fold, beside)

    next_t, half = ocean(
        state, south, north, east_west, exchange_rate, sea_mask, own, got
    )
    order = list(range(tiles - 1, 0, -1))
    arrived = {d: across(half, d) for d in order}
    mine = jnp.concatenate([half] + [arrived[d] for d in range(1, tiles)], axis=0)
    other = lax.ppermute(mine, "sub", swap)
    air_exchange, out_t = backward(slot, block_patch, mine, other, block_weights, advected)
    return (
        jnp.transpose(out_t, (1, 0, 2)),
        jnp.transpose(next_t, (1, 0, 2)),
        air_exchange,
    )


def solution(mesh):
    placed = (
        P("members", None, ("tile", "sub")),
        P("members", ("tile", "sub")),
        P("members", ("tile", "sub")),
        P(("tile", "sub"), None, None),
        P(),
        P(),
        P(("tile", "sub")),
        P("members", "sub", "tile"),
        P("sub", "tile"),
        P("sub", "tile"),
    )
    return jax.shard_map(
        per_device,
        mesh=mesh,
        in_specs=placed,
        out_specs=(
            P("members", None, ("tile", "sub")),
            P("members", "sub", "tile"),
            P("members", ("tile", "sub")),
        ),
        check_vma=False,
    )
```

```python
import functools

import jax
import jax.numpy as jnp
from jax import lax
from jax.experimental import pallas as pl
from jax.experimental.pallas import tpu as pltpu
from jax.sharding import PartitionSpec as P

ASTEPS = 3
NU = 0.2
COUPLE = 0.5
LANES = 128
EDGE = 16
GROUPS = LANES // EDGE
UNROLL = 64

VMEM = pl.BlockSpec(memory_space=pltpu.VMEM)
SMEM = pl.BlockSpec(memory_space=pltpu.SMEM)
ANY = pl.BlockSpec(memory_space=pl.ANY)
HBM = pl.BlockSpec(memory_space=pltpu.HBM)
f32 = jnp.float32
bf16 = jnp.bfloat16


def params(limit):
    return pltpu.CompilerParams(vmem_limit_bytes=limit)


def place():
    sizes = lax.axis_size("tile"), lax.axis_size("sub")
    return lax.axis_index("tile"), lax.axis_index("sub"), *sizes


def is_even():
    tile, sub, _, subs = place()
    return (tile * subs + sub) % 2 == 0


def lane_roll(x, shift):
    length = x.shape[-1]
    shift = shift % length
    return x if shift == 0 else pltpu.roll(x, shift, x.ndim - 1)


def coefficients(c):
    d = 1.0 - c
    return c * d * d * (1.0 / 12.0), c * c * d * (1.0 / 12.0), c * c * (3.0 - 2.0 * c)


def advect(q, right, left, own):
    for _ in range(ASTEPS):
        pair = q + lane_roll(q, -1)
        edge = 8.0 * pair - (lane_roll(pair, 1) + lane_roll(pair, -1))
        flux = right * edge - left * lane_roll(edge, 1) + own * q
        q = q - (flux - lane_roll(flux, 1))
    return q


def pack_kernel(
    tracers, levels, q_hbm, c_hbm, a_ref, b_ref, left_t, right_t, left_c, right_c, sems
):
    span = q_hbm.shape[2]
    copies = [
        pltpu.make_async_copy(src, dst, sems.at[i])
        for i, (src, dst) in enumerate(
            (
                (q_hbm.at[:, :, pl.ds(0, LANES)], left_t),
                (q_hbm.at[:, :, pl.ds(span - LANES, LANES)], right_t),
                (c_hbm.at[:, pl.ds(0, LANES)], left_c),
                (c_hbm.at[:, pl.ds(span - LANES, LANES)], right_c),
            )
        )
    ]
    for copy in copies:
        copy.start()
    for copy in copies:
        copy.wait()
    even = is_even()
    lane = lax.broadcasted_iota(jnp.int32, (levels, LANES), 1)
    pad = pl.cdiv(levels, 8) * 8
    for out, from_left in ((a_ref, jnp.logical_not(even)), (b_ref, even)):
        for part in range(pl.cdiv(tracers + 1, GROUPS)):
            total = jnp.zeros((levels, LANES), f32)
            for group in range(GROUPS):
                item = part * GROUPS + group
                if item > tracers:
                    continue
                low = left_t[item] if item < tracers else left_c[...]
                high = right_t[item] if item < tracers else right_c[...]
                moved = jnp.where(
                    from_left,
                    lane_roll(low, EDGE * group),
                    lane_roll(high, EDGE * (group + 1)),
                )
                total = jnp.where(lane // EDGE == group, moved, total)
            out[part * pad : part * pad + levels, :] = total
        top = pl.cdiv(tracers + 1, GROUPS) * pad
        for item in range(tracers):
            out[top + item : top + item + 1, :] = jnp.where(
                from_left, left_t[item, 0:1, :], right_t[item, 0:1, :]
            )
        out[top + tracers : top + tracers + 1, :] = jnp.where(
            from_left, left_c[0:1, :], right_c[0:1, :]
        )


def pack(tracers_t, courant):
    tracers, levels, span = tracers_t.shape
    pad = pl.cdiv(levels, 8) * 8
    rows = pl.cdiv(tracers + 1, GROUPS) * pad + pl.cdiv(tracers + 1, 8) * 8
    message = jax.ShapeDtypeStruct((rows, LANES), f32)
    return pl.pallas_call(
        functools.partial(pack_kernel, tracers, levels),
        out_shape=(message, message),
        in_specs=[HBM, HBM],
        out_specs=(VMEM, VMEM),
        scratch_shapes=[
            pltpu.VMEM((tracers, levels, LANES), f32),
            pltpu.VMEM((tracers, levels, LANES), f32),
            pltpu.VMEM((levels, LANES), f32),
            pltpu.VMEM((levels, LANES), f32),
            pltpu.SemaphoreType.DMA((4,)),
        ],
        compiler_params=params(56 * 1024 * 1024),
        name="pack_edges",
    )(tracers_t, courant)


def high_low(x):
    high = x.astype(bf16)
    return high, (x - high.astype(f32)).astype(bf16)


def forward_kernel(
    dims, slot_ref, patch_ref, level0, courant0, air, msg_a, msg_b, beside,
    weights_hbm, send_ref, keep_hbm, surface, total, weights, sems, keep_sem,
):
    tracers, span, top = dims
    blocks = weights.shape[0]
    copies = [
        pltpu.make_async_copy(
            weights_hbm.at[pl.ds(i, UNROLL)], weights.at[pl.ds(i, UNROLL)], sems.at[i // UNROLL]
        )
        for i in range(0, blocks, UNROLL)
    ]
    for copy in copies:
        copy.start()
    even = is_even()
    a, b = msg_a[top : top + tracers + 1, :], msg_b[top : top + tracers + 1, :]
    left, right = jnp.where(even, b, a), jnp.where(even, a, b)
    q = jnp.concatenate([left[:tracers], level0[...], right[:tracers]], axis=1)
    c = jnp.concatenate([left[tracers:], courant0[0:1, :], right[tracers:]], axis=1)
    advected = advect(q, *coefficients(c))[:, LANES : LANES + span]
    fields = jnp.concatenate([advected, air[...]], axis=0).astype(bf16)
    for p in range(span // LANES):
        surface[p] = fields[:, p * LANES : (p + 1) * LANES]
    total[...] = jnp.zeros_like(total)
    zero = jnp.zeros(surface.shape[1:], bf16)
    height = zero.shape[0]

    def step(g, carry):
        base = g * UNROLL
        pltpu.make_async_copy(
            weights_hbm.at[pl.ds(base, UNROLL)], weights.at[pl.ds(base, UNROLL)], sems.at[g]
        ).wait()
        products = []
        for u in range(0, UNROLL, 2):
            first, second = surface[patch_ref[base + u]], surface[patch_ref[base + u + 1]]
            rows = jnp.concatenate(
                [jnp.concatenate([first, zero], 1), jnp.concatenate([zero, second], 1)], 0
            )
            pair = weights[pl.ds(base + u, 2)].reshape(2 * LANES, LANES)
            both = jnp.dot(rows, pair, preferred_element_type=f32)
            products += [both[:height], both[height:]]
        for u in range(UNROLL):
            total[slot_ref[base + u]] += products[u]
        return carry

    lax.fori_loop(0, blocks // UNROLL, step, 0)
    half = total.shape[0] // 2
    keep = pltpu.make_async_copy(total.at[pl.ds(0, half)], keep_hbm, keep_sem)
    keep.start()
    send_ref[:half] = total[half:].astype(bf16)
    send_ref[half], send_ref[half + 1] = high_low(beside[...])
    keep.wait()


def forward(slot, patch, level0, courant, air, msg_a, msg_b, beside, weights, rows):
    tracers, span = level0.shape
    levels = courant.shape[0]
    fields = tracers + air.shape[0]
    pad = pl.cdiv(levels, 8) * 8
    top = pl.cdiv(tracers + 1, GROUPS) * pad
    return pl.pallas_call(
        functools.partial(forward_kernel, (tracers, span, top)),
        out_shape=(
            jax.ShapeDtypeStruct((rows // 2 + 2, fields, LANES), bf16),
            jax.ShapeDtypeStruct((rows // 2, fields, LANES), f32),
        ),
        in_specs=[SMEM] * 2 + [VMEM] * 6 + [HBM],
        out_specs=(VMEM, HBM),
        scratch_shapes=[
            pltpu.VMEM((span // LANES, fields, LANES), bf16),
            pltpu.VMEM((rows, fields, LANES), f32),
            pltpu.VMEM(weights.shape, bf16),
            pltpu.SemaphoreType.DMA((weights.shape[0] // UNROLL,)),
            pltpu.SemaphoreType.DMA,
        ],
        compiler_params=params(52 * 1024 * 1024),
        name="blocks_to_rows",
    )(slot, patch, level0, courant, air, msg_a, msg_b, beside, weights)


def with_edges(d):
    return d & (d + 1) == 0


def merge_kernel(chunk, keep, got, state, fold, own_ref, beside_ref, *outs):
    rows, fields, lanes = state.shape
    lane = lax.broadcasted_iota(jnp.int32, (fields, lanes), 1)
    edges = jnp.zeros((fields, lanes), f32)
    for r in range(rows):
        edges = jnp.where(lane == r, lane_roll(state[r], r + 1), edges)
        edges = jnp.where(lane == rows + r, lane_roll(state[r], rows + r), edges)
    more = high_low(edges) + high_low(fold[...])
    own_ref[...] = keep[:chunk] + got[:chunk].astype(f32)
    for d, out in enumerate(outs, 1):
        part = slice(d * chunk, (d + 1) * chunk)
        out[:chunk] = (keep[part] + got[part].astype(f32)).astype(bf16)
        if with_edges(d):
            for i, extra in enumerate(more):
                out[chunk + i] = extra
    last = keep.shape[0]
    beside_ref[...] = got[last].astype(f32) + got[last + 1].astype(f32)


def merge(keep, got, state, fold, chunk):
    rows, fields, lanes = keep.shape
    count = rows // chunk
    return pl.pallas_call(
        functools.partial(merge_kernel, chunk),
        out_shape=(
            jax.ShapeDtypeStruct((chunk, fields, lanes), f32),
            jax.ShapeDtypeStruct((fields, lanes), f32),
        )
        + tuple(
            jax.ShapeDtypeStruct((chunk + 4 * with_edges(d), fields, lanes), bf16)
            for d in range(1, count)
        ),
        in_specs=[VMEM] * 4,
        out_specs=(VMEM,) * (count + 1),
        compiler_params=params((10 if count < 16 else 24) * 1024 * 1024),
        name="merge_cores",
    )(keep, got, state, fold)


def ocean_kernel(count, state, beside, rate, wet, own, *rest):
    got, (next_ref, half_ref) = rest[:count], rest[-2:]
    rows, fields, lanes = state.shape
    lane = lax.broadcasted_iota(jnp.int32, (fields, lanes), 1)
    tile, sub, tiles, subs = place()
    to_east, to_west = tile ^ ((tile + 1) % tiles), tile ^ ((tile + tiles - 1) % tiles)

    def extra(chunk, i):
        return chunk[rows + i].astype(f32) + chunk[rows + i + 1].astype(f32)

    from_east = from_west = jnp.zeros((fields, lanes), f32)
    for d, chunk in enumerate(got, 1):
        if with_edges(d):
            edges = extra(chunk, 0)
            from_east = jnp.where(to_east == d, edges, from_east)
            from_west = jnp.where(to_west == d, edges, from_west)
    south = jnp.where(sub == 0, 0.0, beside[...])
    north = jnp.where(sub == subs - 1, extra(got[-1], 2), beside[...])
    for r in range(rows):
        here = state[r]
        west = jnp.where(lane == 0, lane_roll(from_west, -r), lane_roll(here, 1))
        east = jnp.where(
            lane == lanes - 1, lane_roll(from_east, lanes - 1 - rows - r), lane_roll(here, -1)
        )
        below = state[r - 1] if r else south
        above = state[r + 1] if r < rows - 1 else north
        lateral = west + east + below + above - 4.0 * here
        remapped = own[r]
        for chunk in got:
            remapped = remapped + chunk[r].astype(f32)
        new = here + wet[r : r + 1, :].astype(f32) * (
            rate[r : r + 1, :] * (remapped - here) + NU * lateral
        )
        next_ref[r] = new
        half_ref[r] = new.astype(bf16)


def ocean(state, beside, rate, wet, own, got, after):
    rows, fields, lanes = state.shape
    return pl.pallas_call(
        functools.partial(ocean_kernel, len(got)),
        out_shape=(
            jax.ShapeDtypeStruct(state.shape, f32),
            jax.ShapeDtypeStruct(state.shape, bf16),
        ),
        in_specs=[VMEM] * (5 + len(got)) + [ANY],
        out_specs=(VMEM, VMEM),
        compiler_params=params(8 * 1024 * 1024),
        name="ocean_update",
    )(state, beside, rate, wet, own, *got, after)


def gather_kernel(count, *refs):
    out = refs[-1]
    chunk = refs[0].shape[0]
    for i in range(count):
        out[i * chunk : (i + 1) * chunk] = refs[i][...]


def gather_rows(parts, after):
    chunk, fields, lanes = parts[0].shape
    return pl.pallas_call(
        functools.partial(gather_kernel, len(parts)),
        out_shape=jax.ShapeDtypeStruct((chunk * len(parts), fields, lanes), bf16),
        in_specs=[VMEM] * len(parts) + [ANY],
        out_specs=VMEM,
        compiler_params=params(8 * 1024 * 1024),
        name="gather_rows",
    )(*parts, after)


def advect_kernel(
    tracers, levels, first, group, q_ref, c_ref, msg_a, msg_b, *rest
):
    out_ref, flag_ref, right, left, own, state, lhs, band = rest[-8:]
    even = is_even()
    span = q_ref.shape[2]
    pad = pl.cdiv(levels, 8) * 8
    tiles = span // LANES + 2
    rows = group * pad
    tile = lambda i: slice(i * LANES, (i + 1) * LANES)

    def sides(item):
        start = pl.multiple_of(item // GROUPS * pad, 8)
        shift = EDGE * (item % GROUPS)
        a, b = msg_a[pl.ds(start, levels), :], msg_b[pl.ds(start, levels), :]
        before, after = jnp.where(even, b, a), jnp.where(even, a, b)
        return (
            pltpu.roll(before, (2 * LANES - EDGE - shift) % LANES, 1),
            pltpu.roll(after, (LANES - shift) % LANES, 1),
        )

    @pl.when(pl.program_id(0) == 0)
    def _():
        before, after = sides(tracers)
        c = jnp.concatenate([before, c_ref[...], after], axis=1)
        for ref, value in zip((right, left, own), coefficients(c)):
            ref[...] = jnp.zeros_like(ref)
            for i in range(tiles):
                ref[i, :levels] = value[:, tile(i)]
        state[...] = jnp.zeros_like(state)
        r = lax.broadcasted_iota(jnp.int32, band.shape, 0) % (2 * LANES)
        j = lax.broadcasted_iota(jnp.int32, band.shape, 1)
        column = jnp.where(r < LANES, r, jnp.where(r < LANES + LANES // 2, r, r - 2 * LANES))
        d = column - jnp.where(j < LANES, j, j - LANES - 1)
        weight = jnp.where((d == 0) | (d == 1), 7.0, jnp.where((d == -1) | (d == 2), -1.0, 0.0))
        band[...] = weight.astype(bf16)
        flag_ref[...] = jnp.zeros_like(flag_ref)

    for t in range(group):
        before, after = sides(pl.program_id(0) * group + first + t)
        part = slice(t * pad, t * pad + levels)
        state[0, part] = before
        for i in range(1, tiles - 1):
            state[i, part] = q_ref[t, :, tile(i - 1)]
        state[tiles - 1, part] = after

    lane = lax.broadcasted_iota(jnp.int32, (rows, LANES), 1)
    for _ in range(ASTEPS):
        halves = [high_low(state[i]) for i in range(tiles)]
        for i in range(tiles):
            part = slice(i * rows, (i + 1) * rows)
            for h in range(2):
                lhs[part, tile(2 * h)] = halves[i][h]
                lhs[part, tile(2 * h + 1)] = jnp.where(
                    lane < LANES // 2, halves[min(i + 1, tiles - 1)][h], halves[max(i - 1, 0)][h]
                )
        edges = jnp.dot(lhs[...], band[...], preferred_element_type=f32)
        last = None
        for i in range(tiles):
            edge = edges[i * rows : (i + 1) * rows].reshape(group, pad, 2 * LANES)
            q = state[i]
            flux = (
                right[i] * edge[..., :LANES] - left[i] * edge[..., LANES:]
            ).reshape(rows, LANES) + (own[i] * q.reshape(group, pad, LANES)).reshape(rows, LANES)
            moved = pltpu.roll(flux, 1, 1)
            before = moved if last is None else jnp.where(lane == 0, last, moved)
            state[i] = q - (flux - before)
            last = moved

    for t in range(group):
        for i in range(1, tiles - 1):
            out_ref[t, :, tile(i - 1)] = state[i, t * pad : t * pad + levels]


def advect_some(tracers_t, courant, msg_a, msg_b, first, count, after, into=None):
    tracers, levels, span = tracers_t.shape
    group = 2 if count % 2 == 0 and first % 2 == 0 else 1
    tiles, pad = span // LANES + 2, pl.cdiv(levels, 8) * 8
    whole = lambda shape: pl.BlockSpec(shape, lambda i: (0,) * len(shape))
    block = pl.BlockSpec((group, levels, span), lambda i: (i + first // group, 0, 0))
    more = [after] if into is None else [after, into]
    return pl.pallas_call(
        functools.partial(advect_kernel, tracers, levels, first, group),
        grid=(count // group,),
        out_shape=(
            jax.ShapeDtypeStruct(tracers_t.shape, f32),
            jax.ShapeDtypeStruct((8, LANES), f32),
        ),
        in_specs=[
            block,
            whole(courant.shape),
            whole(msg_a.shape),
            whole(msg_b.shape),
        ]
        + [ANY] * len(more),
        out_specs=(block, whole((8, LANES))),
        input_output_aliases={} if into is None else {5: 0},
        scratch_shapes=[pltpu.VMEM((tiles, pad, LANES), f32)] * 3
        + [
            pltpu.VMEM((tiles, group * pad, LANES), f32),
            pltpu.VMEM((tiles * group * pad, 4 * LANES), bf16),
            pltpu.VMEM((4 * LANES, 2 * LANES), bf16),
        ],
        compiler_params=params(12 * 1024 * 1024),
        cost_estimate=pl.CostEstimate(
            flops=200 * count * levels * span,
            bytes_accessed=8 * count * levels * span,
            transcendentals=0,
        ),
        name="advect_levels",
    )(tracers_t, courant, msg_a, msg_b, *more)


def backward_kernel(
    slot_ref, patch_ref, mine, other, weights_hbm, advected_hbm, air_ref, out_hbm,
    rows, total, bottom, sem, weights, sems,
):
    copies = [
        pltpu.make_async_copy(
            weights_hbm.at[pl.ds(i, UNROLL)], weights.at[pl.ds(i, UNROLL)], sems.at[i // UNROLL]
        )
        for i in range(0, weights.shape[0], UNROLL)
    ]
    for copy in copies:
        copy.start()
    fetch = pltpu.make_async_copy(advected_hbm.at[:, pl.ds(0, 8), :], bottom, sem)
    fetch.start()
    tracers, _, span = bottom.shape
    blocks = weights.shape[0]
    half, fields, _ = mine.shape
    rows[:half] = mine[...]
    rows[half:] = other[...]
    total[...] = jnp.zeros_like(total)

    def step(g, carry):
        base = g * UNROLL
        pltpu.make_async_copy(
            weights_hbm.at[pl.ds(base, UNROLL)], weights.at[pl.ds(base, UNROLL)], sems.at[g]
        ).wait()
        products = []
        for u in range(0, UNROLL, 2):
            both = lax.dot_general(
                jnp.concatenate([rows[slot_ref[base + u]], rows[slot_ref[base + u + 1]]], 0),
                weights[pl.ds(base + u, 2)].reshape(2 * LANES, LANES),
                (((1,), (1,)), ((), ())),
                preferred_element_type=f32,
            )
            products += [both[:fields, :LANES], both[fields:, LANES:]]
        for u in range(UNROLL):
            total[patch_ref[base + u]] += products[u]
        return carry

    lax.fori_loop(0, blocks // UNROLL, step, 0)
    fetch.wait()
    for p in range(span // LANES):
        part = slice(p * LANES, (p + 1) * LANES)
        exchange = total[p]
        air_ref[:, part] = exchange
        bottom[:, 0, part] += COUPLE * exchange[:tracers]
    store = pltpu.make_async_copy(bottom, out_hbm.at[:, pl.ds(0, 8), :], sem)
    store.start()
    store.wait()


def backward(slot, patch, mine, other, weights, advected):
    tracers, levels, span = advected.shape
    half, fields, lanes = mine.shape
    return pl.pallas_call(
        backward_kernel,
        out_shape=(
            jax.ShapeDtypeStruct((fields, span), f32),
            jax.ShapeDtypeStruct(advected.shape, f32),
        ),
        in_specs=[SMEM, SMEM, VMEM, VMEM, HBM, HBM],
        out_specs=(VMEM, HBM),
        input_output_aliases={5: 1},
        scratch_shapes=[
            pltpu.VMEM((2 * half, fields, lanes), bf16),
            pltpu.VMEM((span // lanes, fields, lanes), f32),
            pltpu.VMEM((tracers, 8, span), f32),
            pltpu.SemaphoreType.DMA,
            pltpu.VMEM(weights.shape, bf16),
            pltpu.SemaphoreType.DMA((weights.shape[0] // UNROLL,)),
        ],
        compiler_params=params(52 * 1024 * 1024),
        name="rows_to_columns",
    )(slot, patch, mine, other, weights, advected)


def per_device(
    tracers,
    courant,
    air_surface,
    block_weights,
    block_dest,
    block_row,
    block_patch,
    ocean_state,
    exchange_rate,
    sea_mask,
):
    tiles, subs = lax.axis_size("tile"), lax.axis_size("sub")
    devices = tiles * subs
    my_tile, my_sub = lax.axis_index("tile"), lax.axis_index("sub")
    my_index = my_tile * subs + my_sub
    blocks = block_weights.shape[0]
    fields, ocean_rows, lanes = ocean_state.shape
    flat = ("tile", "sub")
    tracers_t = jnp.transpose(tracers, (1, 0, 2))
    pack_a, pack_b = pack(tracers_t, courant)
    msg_b = lax.ppermute(
        pack_b, flat, [(i, (i + 1 if i % 2 else i - 1) % devices) for i in range(devices)]
    )
    msg_a = lax.ppermute(pack_a, flat, [(i, i ^ 1) for i in range(devices)])

    start = my_index * blocks
    dest = lax.dynamic_slice(block_dest.reshape(-1), (start,), (blocks,))
    row = lax.dynamic_slice(block_row, (start,), (blocks,))
    chunk_of = ((dest // subs) ^ my_tile) + tiles * ((dest % subs + subs - my_sub) % subs)
    slot = chunk_of * ocean_rows + row

    state = jnp.transpose(ocean_state, (1, 0, 2))
    sign = jnp.where(jnp.arange(fields) >= fields - 2, -1.0, 1.0).astype(f32)[:, None]
    fold = sign * ocean_state[:, -1, ::-1]
    beside = jnp.where(my_sub == subs - 1, ocean_state[:, 0], ocean_state[:, -1])

    send, keep = forward(
        slot, block_patch, tracers[0], courant, air_surface, msg_a, msg_b, beside,
        block_weights, devices * ocean_rows,
    )
    swap = [(0, 1), (1, 0)]
    got = lax.ppermute(send, "sub", swap)
    own, beside, *partial = merge(keep, got, state, fold, ocean_rows)
    across = lambda x, d: lax.ppermute(x, "tile", [(i, i ^ d) for i in range(tiles)])
    got = [across(x, d) for d, x in enumerate(partial, 1)]

    count = tracers.shape[1] // 2
    some, flag = advect_some(tracers_t, courant, msg_a, msg_b, 0, count, own)
    next_ocean, half = ocean(
        state, beside, exchange_rate, sea_mask, own, got, flag
    )

    first = [1, 2, 3] + list(range(tiles - 1, 5, -1))
    arrived = {d: across(half, d) for d in first}
    for d, behind in ((5, 1), (4, 2)):
        ready, _ = lax.optimization_barrier((half, arrived[behind]))
        arrived[d] = across(ready, d)
    advected, flag = advect_some(
        tracers_t, courant, msg_a, msg_b, count, tracers.shape[1] - count, half, some
    )
    mine = gather_rows([half] + [arrived[d] for d in range(1, tiles)], flag)
    other = lax.ppermute(mine, "sub", swap)
    air_exchange, out_t = backward(slot, block_patch, mine, other, block_weights, advected)
    return jnp.transpose(out_t, (1, 0, 2)), jnp.transpose(next_ocean, (1, 0, 2)), air_exchange


def solution(mesh):
    placed = (
        P("members", None, ("tile", "sub")),
        P("members", ("tile", "sub")),
        P("members", ("tile", "sub")),
        P(("tile", "sub"), None, None),
        P(),
        P(),
        P(("tile", "sub")),
        P("members", "sub", "tile"),
        P("sub", "tile"),
        P("sub", "tile"),
    )
    return jax.shard_map(
        per_device,
        mesh=mesh,
        in_specs=placed,
        out_specs=(
            P("members", None, ("tile", "sub")),
            P("members", "sub", "tile"),
            P("members", ("tile", "sub")),
        ),
        check_vma=False,
    )
```

```python
import functools

import jax
import jax.numpy as jnp
from jax import lax
from jax.experimental import pallas as pl
from jax.experimental.pallas import tpu as pltpu
from jax.sharding import PartitionSpec as P

ASTEPS = 3
NU = 0.2
COUPLE = 0.5
LANES = 128
EDGE = 16
GROUPS = LANES // EDGE
UNROLL = 64
SPLIT = (6, 2, 4)

VMEM = pl.BlockSpec(memory_space=pltpu.VMEM)
SMEM = pl.BlockSpec(memory_space=pltpu.SMEM)
ANY = pl.BlockSpec(memory_space=pl.ANY)
HBM = pl.BlockSpec(memory_space=pltpu.HBM)
f32 = jnp.float32
bf16 = jnp.bfloat16


def params(limit):
    return pltpu.CompilerParams(vmem_limit_bytes=limit)


def place():
    sizes = lax.axis_size("tile"), lax.axis_size("sub")
    return lax.axis_index("tile"), lax.axis_index("sub"), *sizes


def is_even():
    tile, sub, _, subs = place()
    return (tile * subs + sub) % 2 == 0


def lane_roll(x, shift):
    length = x.shape[-1]
    shift = shift % length
    return x if shift == 0 else pltpu.roll(x, shift, x.ndim - 1)


def coefficients(c):
    d = 1.0 - c
    return c * d * d * (1.0 / 12.0), c * c * d * (1.0 / 12.0), c * c * (3.0 - 2.0 * c)


def advect(q, right, left, own):
    for _ in range(ASTEPS):
        pair = q + lane_roll(q, -1)
        edge = 8.0 * pair - (lane_roll(pair, 1) + lane_roll(pair, -1))
        flux = right * edge - left * lane_roll(edge, 1) + own * q
        q = q - (flux - lane_roll(flux, 1))
    return q


def pack_kernel(
    tracers, levels, q_hbm, c_hbm, a_ref, b_ref, left_t, right_t, left_c, right_c, sems
):
    span = q_hbm.shape[2]
    copies = [
        pltpu.make_async_copy(src, dst, sems.at[i])
        for i, (src, dst) in enumerate(
            (
                (q_hbm.at[:, :, pl.ds(0, LANES)], left_t),
                (q_hbm.at[:, :, pl.ds(span - LANES, LANES)], right_t),
                (c_hbm.at[:, pl.ds(0, LANES)], left_c),
                (c_hbm.at[:, pl.ds(span - LANES, LANES)], right_c),
            )
        )
    ]
    for copy in copies:
        copy.start()
    for copy in copies:
        copy.wait()
    even = is_even()
    lane = lax.broadcasted_iota(jnp.int32, (levels, LANES), 1)
    pad = pl.cdiv(levels, 8) * 8
    for out, from_left in ((a_ref, jnp.logical_not(even)), (b_ref, even)):
        for part in range(pl.cdiv(tracers + 1, GROUPS)):
            total = jnp.zeros((levels, LANES), f32)
            for group in range(GROUPS):
                item = part * GROUPS + group
                if item > tracers:
                    continue
                low = left_t[item] if item < tracers else left_c[...]
                high = right_t[item] if item < tracers else right_c[...]
                moved = jnp.where(
                    from_left,
                    lane_roll(low, EDGE * group),
                    lane_roll(high, EDGE * (group + 1)),
                )
                total = jnp.where(lane // EDGE == group, moved, total)
            out[part * pad : part * pad + levels, :] = total
        top = pl.cdiv(tracers + 1, GROUPS) * pad
        for item in range(tracers):
            out[top + item : top + item + 1, :] = jnp.where(
                from_left, left_t[item, 0:1, :], right_t[item, 0:1, :]
            )
        out[top + tracers : top + tracers + 1, :] = jnp.where(
            from_left, left_c[0:1, :], right_c[0:1, :]
        )


def pack(tracers_t, courant):
    tracers, levels, span = tracers_t.shape
    pad = pl.cdiv(levels, 8) * 8
    rows = pl.cdiv(tracers + 1, GROUPS) * pad + pl.cdiv(tracers + 1, 8) * 8
    message = jax.ShapeDtypeStruct((rows, LANES), f32)
    return pl.pallas_call(
        functools.partial(pack_kernel, tracers, levels),
        out_shape=(message, message),
        in_specs=[HBM, HBM],
        out_specs=(VMEM, VMEM),
        scratch_shapes=[
            pltpu.VMEM((tracers, levels, LANES), f32),
            pltpu.VMEM((tracers, levels, LANES), f32),
            pltpu.VMEM((levels, LANES), f32),
            pltpu.VMEM((levels, LANES), f32),
            pltpu.SemaphoreType.DMA((4,)),
        ],
        compiler_params=params(56 * 1024 * 1024),
        name="pack_edges",
    )(tracers_t, courant)


def slot_kernel(chunk, dest_ref, row_ref, _, slot_ref, back_ref):
    tile, sub, tiles, subs = place()
    count = slot_ref.shape[0]
    mine = pl.ds((tile * subs + sub) * count, count)
    dest = dest_ref[mine, :]
    apart = (dest // subs) ^ tile
    core = (dest % subs + subs - sub) % subs * tiles
    row = row_ref[mine, :]
    slot_ref[...] = (core + apart) * chunk + row
    back_ref[...] = (core + apart % 2 * (tiles // 2) + apart // 2) * chunk + row


def find_slots(dest, row, weights, chunk):
    blocks = weights.shape[0]
    whole = (dest.size // LANES, LANES)
    return pl.pallas_call(
        functools.partial(slot_kernel, chunk),
        out_shape=(jax.ShapeDtypeStruct((blocks // LANES, LANES), jnp.int32),) * 2,
        in_specs=[VMEM, VMEM, VMEM],
        out_specs=(VMEM, VMEM),
        compiler_params=params(28 * 1024 * 1024),
        name="find_slots",
    )(dest.reshape(whole), row.reshape(whole), weights)


def high_low(x):
    high = x.astype(bf16)
    return high, (x - high.astype(f32)).astype(bf16)


def forward_kernel(
    dims, slot_ref, patch_ref, level0, courant0, air, msg_a, msg_b, state, weights,
    send_ref, keep_ref, surface, total,
):
    tracers, span, top = dims
    blocks = weights.shape[0]
    even = is_even()
    a, b = msg_a[top : top + tracers + 1, :], msg_b[top : top + tracers + 1, :]
    left, right = jnp.where(even, b, a), jnp.where(even, a, b)
    q = jnp.concatenate([left[:tracers], level0[...], right[:tracers]], axis=1)
    c = jnp.concatenate([left[tracers:], courant0[0:1, :], right[tracers:]], axis=1)
    advected = advect(q, *coefficients(c))[:, LANES : LANES + span]
    fields = jnp.concatenate([advected, air[...]], axis=0).astype(bf16)
    for p in range(span // LANES):
        surface[p] = fields[:, p * LANES : (p + 1) * LANES]
    total[...] = jnp.zeros_like(total)
    zero = jnp.zeros(surface.shape[1:], bf16)
    height = zero.shape[0]

    def step(g, carry):
        base = g * UNROLL
        products = []
        for u in range(0, UNROLL, 2):
            first, second = surface[patch_ref[base + u]], surface[patch_ref[base + u + 1]]
            rows = jnp.concatenate(
                [jnp.concatenate([first, zero], 1), jnp.concatenate([zero, second], 1)], 0
            )
            pair = weights[pl.ds(base + u, 2)].reshape(2 * LANES, LANES)
            both = jnp.dot(rows, pair, preferred_element_type=f32)
            products += [both[:height], both[height:]]
        for u in range(UNROLL):
            total[slot_ref[(base + u) // LANES, (base + u) % LANES]] += products[u]
        return carry

    lax.fori_loop(0, blocks // UNROLL, step, 0)
    half = total.shape[0] // 2
    keep_ref[...] = total[:half]
    send_ref[:half] = total[half:].astype(bf16)
    _, sub, _, subs = place()
    beside = jnp.where(sub == subs - 1, state[0], state[state.shape[0] - 1])
    send_ref[half], send_ref[half + 1] = high_low(beside)


def forward(slot, patch, level0, courant, air, msg_a, msg_b, state, weights, rows):
    tracers, span = level0.shape
    levels = courant.shape[0]
    fields = tracers + air.shape[0]
    pad = pl.cdiv(levels, 8) * 8
    top = pl.cdiv(tracers + 1, GROUPS) * pad
    return pl.pallas_call(
        functools.partial(forward_kernel, (tracers, span, top)),
        out_shape=(
            jax.ShapeDtypeStruct((rows // 2 + 2, fields, LANES), bf16),
            jax.ShapeDtypeStruct((rows // 2, fields, LANES), f32),
        ),
        in_specs=[SMEM] * 2 + [VMEM] * 7,
        out_specs=(VMEM, VMEM),
        scratch_shapes=[
            pltpu.VMEM((span // LANES, fields, LANES), bf16),
            pltpu.VMEM((rows, fields, LANES), f32),
        ],
        compiler_params=params(28 * 1024 * 1024),
        name="blocks_to_rows",
    )(slot, patch, level0, courant, air, msg_a, msg_b, state, weights)


def with_edges(d):
    return d & (d + 1) == 0


def merge_kernel(chunk, keep, got, state, own_ref, beside_ref, *outs):
    rows, fields, lanes = state.shape
    lane = lax.broadcasted_iota(jnp.int32, (fields, lanes), 1)
    edges = jnp.zeros((fields, lanes), f32)
    for r in range(rows):
        edges = jnp.where(lane == r, lane_roll(state[r], r + 1), edges)
        edges = jnp.where(lane == rows + r, lane_roll(state[r], rows + r), edges)
    sign = jnp.where(lax.broadcasted_iota(jnp.int32, (fields, lanes), 0) < fields - 2, 1.0, -1.0)
    mirror = lax.broadcasted_iota(jnp.int32, (lanes, lanes), 0) + lax.broadcasted_iota(
        jnp.int32, (lanes, lanes), 1
    )
    mirror = jnp.where(mirror == lanes - 1, 1.0, 0.0).astype(bf16)
    fold = [
        (jnp.dot(part, mirror, preferred_element_type=f32) * sign).astype(bf16)
        for part in high_low(state[rows - 1])
    ]
    more = [*high_low(edges), *fold]
    own_ref[...] = keep[:chunk] + got[:chunk].astype(f32)
    for d, out in enumerate(outs, 1):
        part = slice(d * chunk, (d + 1) * chunk)
        out[:chunk] = (keep[part] + got[part].astype(f32)).astype(bf16)
        if with_edges(d):
            for i, extra in enumerate(more):
                out[chunk + i] = extra
    last = keep.shape[0]
    beside_ref[...] = got[last].astype(f32) + got[last + 1].astype(f32)


def merge(keep, got, state, chunk):
    rows, fields, lanes = keep.shape
    count = rows // chunk
    return pl.pallas_call(
        functools.partial(merge_kernel, chunk),
        out_shape=(
            jax.ShapeDtypeStruct((chunk, fields, lanes), f32),
            jax.ShapeDtypeStruct((fields, lanes), f32),
        )
        + tuple(
            jax.ShapeDtypeStruct((chunk + 4 * with_edges(d), fields, lanes), bf16)
            for d in range(1, count)
        ),
        in_specs=[VMEM] * 3,
        out_specs=(VMEM,) * (count + 1),
        compiler_params=params((10 if count < 16 else 24) * 1024 * 1024),
        name="merge_cores",
    )(keep, got, state)


def ocean_kernel(count, state, beside, rate, wet, own, *rest):
    got, (next_ref, half_ref) = rest[:count], rest[-2:]
    rows, fields, lanes = state.shape
    lane = lax.broadcasted_iota(jnp.int32, (fields, lanes), 1)
    tile, sub, tiles, subs = place()
    to_east, to_west = tile ^ ((tile + 1) % tiles), tile ^ ((tile + tiles - 1) % tiles)

    def extra(chunk, i):
        return chunk[rows + i].astype(f32) + chunk[rows + i + 1].astype(f32)

    from_east = from_west = jnp.zeros((fields, lanes), f32)
    for d, chunk in enumerate(got, 1):
        if with_edges(d):
            edges = extra(chunk, 0)
            from_east = jnp.where(to_east == d, edges, from_east)
            from_west = jnp.where(to_west == d, edges, from_west)
    south = jnp.where(sub == 0, 0.0, beside[...])
    north = jnp.where(sub == subs - 1, extra(got[-1], 2), beside[...])
    for r in range(rows):
        here = state[r]
        west = jnp.where(lane == 0, lane_roll(from_west, -r), lane_roll(here, 1))
        east = jnp.where(
            lane == lanes - 1, lane_roll(from_east, lanes - 1 - rows - r), lane_roll(here, -1)
        )
        below = state[r - 1] if r else south
        above = state[r + 1] if r < rows - 1 else north
        lateral = west + east + below + above - 4.0 * here
        remapped = own[r]
        for chunk in got:
            remapped = remapped + chunk[r].astype(f32)
        new = here + wet[r : r + 1, :].astype(f32) * (
            rate[r : r + 1, :] * (remapped - here) + NU * lateral
        )
        next_ref[r] = new
        half_ref[r] = new.astype(bf16)


def ocean(state, beside, rate, wet, own, got, after):
    rows, fields, lanes = state.shape
    return pl.pallas_call(
        functools.partial(ocean_kernel, len(got)),
        out_shape=(
            jax.ShapeDtypeStruct(state.shape, f32),
            jax.ShapeDtypeStruct(state.shape, bf16),
        ),
        in_specs=[VMEM] * (5 + len(got)) + [ANY],
        out_specs=(VMEM, VMEM),
        compiler_params=params(8 * 1024 * 1024),
        name="ocean_update",
    )(state, beside, rate, wet, own, *got, after)


def gather_kernel(count, *refs):
    out = refs[-1]
    chunk = refs[0].shape[0]
    for i in range(count):
        out[i * chunk : (i + 1) * chunk] = refs[i][...]


def gather_rows(parts, after):
    chunk, fields, lanes = parts[0].shape
    return pl.pallas_call(
        functools.partial(gather_kernel, len(parts)),
        out_shape=jax.ShapeDtypeStruct((chunk * len(parts), fields, lanes), bf16),
        in_specs=[VMEM] * len(parts) + [ANY],
        out_specs=VMEM,
        compiler_params=params(8 * 1024 * 1024),
        name="gather_rows",
    )(*parts, after)


def advect_kernel(
    tracers, levels, first, group, q_ref, c_ref, msg_a, msg_b, *rest
):
    out_ref, flag_ref, right, left, own, state, lhs, band = rest[-8:]
    even = is_even()
    span = q_ref.shape[2]
    pad = pl.cdiv(levels, 8) * 8
    tiles = span // LANES + 2
    rows = group * pad
    tile = lambda i: slice(i * LANES, (i + 1) * LANES)

    def sides(item):
        start = pl.multiple_of(item // GROUPS * pad, 8)
        shift = EDGE * (item % GROUPS)
        a, b = msg_a[pl.ds(start, levels), :], msg_b[pl.ds(start, levels), :]
        before, after = jnp.where(even, b, a), jnp.where(even, a, b)
        return (
            pltpu.roll(before, (2 * LANES - EDGE - shift) % LANES, 1),
            pltpu.roll(after, (LANES - shift) % LANES, 1),
        )

    @pl.when(pl.program_id(0) == 0)
    def _():
        before, after = sides(tracers)
        c = jnp.concatenate([before, c_ref[...], after], axis=1)
        for ref, value in zip((right, left, own), coefficients(c)):
            ref[...] = jnp.zeros_like(ref)
            for i in range(tiles):
                ref[i, :levels] = value[:, tile(i)]
        state[...] = jnp.zeros_like(state)
        r = lax.broadcasted_iota(jnp.int32, band.shape, 0) % (2 * LANES)
        j = lax.broadcasted_iota(jnp.int32, band.shape, 1)
        column = jnp.where(r < LANES, r, jnp.where(r < LANES + LANES // 2, r, r - 2 * LANES))
        d = column - jnp.where(j < LANES, j, j - LANES - 1)
        weight = jnp.where((d == 0) | (d == 1), 7.0, jnp.where((d == -1) | (d == 2), -1.0, 0.0))
        band[...] = weight.astype(bf16)
        flag_ref[...] = jnp.zeros_like(flag_ref)

    for t in range(group):
        before, after = sides(pl.program_id(0) * group + first + t)
        part = slice(t * pad, t * pad + levels)
        state[0, part] = before
        for i in range(1, tiles - 1):
            state[i, part] = q_ref[t, :, tile(i - 1)]
        state[tiles - 1, part] = after

    lane = lax.broadcasted_iota(jnp.int32, (rows, LANES), 1)
    for _ in range(ASTEPS):
        halves = [high_low(state[i]) for i in range(tiles)]
        for i in range(tiles):
            part = slice(i * rows, (i + 1) * rows)
            for h in range(2):
                lhs[part, tile(2 * h)] = halves[i][h]
                lhs[part, tile(2 * h + 1)] = jnp.where(
                    lane < LANES // 2, halves[min(i + 1, tiles - 1)][h], halves[max(i - 1, 0)][h]
                )
        edges = jnp.dot(lhs[...], band[...], preferred_element_type=f32)
        last = None
        for i in range(tiles):
            edge = edges[i * rows : (i + 1) * rows].reshape(group, pad, 2 * LANES)
            q = state[i]
            flux = (
                right[i] * edge[..., :LANES] - left[i] * edge[..., LANES:]
            ).reshape(rows, LANES) + (own[i] * q.reshape(group, pad, LANES)).reshape(rows, LANES)
            moved = pltpu.roll(flux, 1, 1)
            before = moved if last is None else jnp.where(lane == 0, last, moved)
            state[i] = q - (flux - before)
            last = moved

    for t in range(group):
        for i in range(1, tiles - 1):
            out_ref[t, :, tile(i - 1)] = state[i, t * pad : t * pad + levels]


def advect_some(tracers_t, courant, msg_a, msg_b, first, count, after, into=None):
    tracers, levels, span = tracers_t.shape
    group = 2 if count % 2 == 0 and first % 2 == 0 else 1
    tiles, pad = span // LANES + 2, pl.cdiv(levels, 8) * 8
    whole = lambda shape: pl.BlockSpec(shape, lambda i: (0,) * len(shape))
    block = pl.BlockSpec((group, levels, span), lambda i: (i + first // group, 0, 0))
    more = [after] if into is None else [after, into]
    return pl.pallas_call(
        functools.partial(advect_kernel, tracers, levels, first, group),
        grid=(count // group,),
        out_shape=(
            jax.ShapeDtypeStruct(tracers_t.shape, f32),
            jax.ShapeDtypeStruct((8, LANES), f32),
        ),
        in_specs=[
            block,
            whole(courant.shape),
            whole(msg_a.shape),
            whole(msg_b.shape),
        ]
        + [ANY] * len(more),
        out_specs=(block, whole((8, LANES))),
        input_output_aliases={} if into is None else {5: 0},
        scratch_shapes=[pltpu.VMEM((tiles, pad, LANES), f32)] * 3
        + [
            pltpu.VMEM((tiles, group * pad, LANES), f32),
            pltpu.VMEM((tiles * group * pad, 4 * LANES), bf16),
            pltpu.VMEM((4 * LANES, 2 * LANES), bf16),
        ],
        compiler_params=params(12 * 1024 * 1024),
        cost_estimate=pl.CostEstimate(
            flops=200 * count * levels * span,
            bytes_accessed=8 * count * levels * span,
            transcendentals=0,
        ),
        name="advect_levels",
    )(tracers_t, courant, msg_a, msg_b, *more)


def backward_kernel(
    slot_ref, patch_ref, even, odd, even_other, odd_other, weights, advected_hbm, air_hbm, out_hbm,
    rows, total, bottom, air, sem, air_sem,
):
    fetch = pltpu.make_async_copy(advected_hbm.at[:, pl.ds(0, 8), :], bottom, sem)
    fetch.start()
    tracers, _, span = bottom.shape
    blocks = weights.shape[0]
    part, fields, _ = even.shape
    for i, some in enumerate((even, odd, even_other, odd_other)):
        rows[i * part : (i + 1) * part] = some[...]
    total[...] = jnp.zeros_like(total)
    slot_of = lambda b: slot_ref[b // LANES, b % LANES]

    def step(g, carry):
        base = g * UNROLL
        products = []
        for u in range(0, UNROLL, 2):
            both = lax.dot_general(
                jnp.concatenate([rows[slot_of(base + u)], rows[slot_of(base + u + 1)]], 0),
                weights[pl.ds(base + u, 2)].reshape(2 * LANES, LANES),
                (((1,), (1,)), ((), ())),
                preferred_element_type=f32,
            )
            products += [both[:fields, :LANES], both[fields:, LANES:]]
        for u in range(UNROLL):
            total[patch_ref[base + u]] += products[u]
        return carry

    lax.fori_loop(0, blocks // UNROLL, step, 0)
    fetch.wait()
    for p in range(span // LANES):
        part = slice(p * LANES, (p + 1) * LANES)
        exchange = total[p]
        air[:, part] = exchange
        bottom[:, 0, part] += COUPLE * exchange[:tracers]
    stores = (
        pltpu.make_async_copy(bottom, out_hbm.at[:, pl.ds(0, 8), :], sem),
        pltpu.make_async_copy(air, air_hbm, air_sem),
    )
    for store in stores:
        store.start()
    for store in stores:
        store.wait()


def backward(slot, patch, parts, weights, advected):
    tracers, levels, span = advected.shape
    part, fields, lanes = parts[0].shape
    return pl.pallas_call(
        backward_kernel,
        out_shape=(
            jax.ShapeDtypeStruct((fields, span), f32),
            jax.ShapeDtypeStruct(advected.shape, f32),
        ),
        in_specs=[SMEM, SMEM] + [VMEM] * 5 + [HBM],
        out_specs=(HBM, HBM),
        input_output_aliases={7: 1},
        scratch_shapes=[
            pltpu.VMEM((4 * part, fields, lanes), bf16),
            pltpu.VMEM((span // lanes, fields, lanes), f32),
            pltpu.VMEM((tracers, 8, span), f32),
            pltpu.VMEM((fields, span), f32),
            pltpu.SemaphoreType.DMA,
            pltpu.SemaphoreType.DMA,
        ],
        compiler_params=params(16 * 1024 * 1024),
        name="rows_to_columns",
    )(slot, patch, *parts, weights, advected)


def per_device(
    tracers,
    courant,
    air_surface,
    block_weights,
    block_dest,
    block_row,
    block_patch,
    ocean_state,
    exchange_rate,
    sea_mask,
):
    tiles, subs = lax.axis_size("tile"), lax.axis_size("sub")
    devices = tiles * subs
    ocean_rows = ocean_state.shape[1]
    flat = ("tile", "sub")
    tracers_t = jnp.transpose(tracers, (1, 0, 2))
    pack_a, pack_b = pack(tracers_t, courant)
    msg_b = lax.ppermute(
        pack_b, flat, [(i, (i + 1 if i % 2 else i - 1) % devices) for i in range(devices)]
    )
    msg_a = lax.ppermute(pack_a, flat, [(i, i ^ 1) for i in range(devices)])

    slot, slot_back = find_slots(block_dest, block_row, block_weights, ocean_rows)
    state = jnp.transpose(ocean_state, (1, 0, 2))
    send, keep = forward(
        slot, block_patch, tracers[0], courant, air_surface, msg_a, msg_b, state,
        block_weights, devices * ocean_rows,
    )
    swap = [(0, 1), (1, 0)]
    got = lax.ppermute(send, "sub", swap)
    own, beside, *partial = merge(keep, got, state, ocean_rows)
    across = lambda x, d: lax.ppermute(x, "tile", [(i, i ^ d) for i in range(tiles)])
    got = [across(x, d) for d, x in enumerate(partial, 1)]

    first, second, third = SPLIT
    advance = functools.partial(advect_some, tracers_t, courant, msg_a, msg_b)
    some, flag = advance(0, first, own)
    next_ocean, half = ocean(
        state, beside, exchange_rate, sea_mask, own, got, flag
    )

    arrived = [across(half, d) for d in range(tiles - 2, 0, -2)]
    some, flag = advance(first, second, half, some)
    even = gather_rows([half] + arrived[::-1], flag)
    odd = across(even, 1)
    even_other = lax.ppermute(even, "sub", swap)
    advected, flag = advance(first + second, third, even, some)
    odd = gather_rows([odd], flag)
    odd_other = lax.ppermute(odd, "sub", swap)
    air_exchange, out_t = backward(
        slot_back, block_patch, (even, odd, even_other, odd_other), block_weights, advected
    )
    return jnp.transpose(out_t, (1, 0, 2)), jnp.transpose(next_ocean, (1, 0, 2)), air_exchange


def solution(mesh):
    placed = (
        P("members", None, ("tile", "sub")),
        P("members", ("tile", "sub")),
        P("members", ("tile", "sub")),
        P(("tile", "sub"), None, None),
        P(),
        P(),
        P(("tile", "sub")),
        P("members", "sub", "tile"),
        P("sub", "tile"),
        P("sub", "tile"),
    )
    return jax.shard_map(
        per_device,
        mesh=mesh,
        in_specs=placed,
        out_specs=(
            P("members", None, ("tile", "sub")),
            P("members", "sub", "tile"),
            P("members", ("tile", "sub")),
        ),
        check_vma=False,
    )
```

```python
import functools

import jax
import jax.numpy as jnp
from jax import lax
from jax.experimental import pallas as pl
from jax.experimental.pallas import tpu as pltpu
from jax.sharding import PartitionSpec as P

ASTEPS = 3
NU = 0.2
COUPLE = 0.5
LANES = 128
EDGE = 16
GROUPS = LANES // EDGE
UNROLL = 64
GROUP = 4
SETS = 2

VMEM = pl.BlockSpec(memory_space=pltpu.VMEM)
SMEM = pl.BlockSpec(memory_space=pltpu.SMEM)
ANY = pl.BlockSpec(memory_space=pl.ANY)
HBM = pl.BlockSpec(memory_space=pltpu.HBM)
f32 = jnp.float32
bf16 = jnp.bfloat16


def params(limit):
    return pltpu.CompilerParams(vmem_limit_bytes=limit)


def place():
    sizes = lax.axis_size("tile"), lax.axis_size("sub")
    return lax.axis_index("tile"), lax.axis_index("sub"), *sizes


def is_even():
    tile, sub, _, subs = place()
    return (tile * subs + sub) % 2 == 0


def lane_roll(x, shift):
    length = x.shape[-1]
    shift = shift % length
    return x if shift == 0 else pltpu.roll(x, shift, x.ndim - 1)


def coefficients(c):
    d = 1.0 - c
    return c * d * d * (1.0 / 12.0), c * c * d * (1.0 / 12.0), c * c * (3.0 - 2.0 * c)


def advect(q, right, left, own):
    for _ in range(ASTEPS):
        pair = q + lane_roll(q, -1)
        edge = 8.0 * pair - (lane_roll(pair, 1) + lane_roll(pair, -1))
        flux = right * edge - left * lane_roll(edge, 1) + own * q
        q = q - (flux - lane_roll(flux, 1))
    return q


def pack_kernel(
    tracers, levels, q_hbm, c_hbm, a_ref, b_ref, left_t, right_t, left_c, right_c, sems
):
    span = q_hbm.shape[2]
    copies = [
        pltpu.make_async_copy(src, dst, sems.at[i])
        for i, (src, dst) in enumerate(
            (
                (q_hbm.at[:, :, pl.ds(0, LANES)], left_t),
                (q_hbm.at[:, :, pl.ds(span - LANES, LANES)], right_t),
                (c_hbm.at[:, pl.ds(0, LANES)], left_c),
                (c_hbm.at[:, pl.ds(span - LANES, LANES)], right_c),
            )
        )
    ]
    for copy in copies:
        copy.start()
    for copy in copies:
        copy.wait()
    even = is_even()
    lane = lax.broadcasted_iota(jnp.int32, (levels, LANES), 1)
    pad = pl.cdiv(levels, 8) * 8
    for out, from_left in ((a_ref, jnp.logical_not(even)), (b_ref, even)):
        for part in range(pl.cdiv(tracers + 1, GROUPS)):
            total = jnp.zeros((levels, LANES), f32)
            for group in range(GROUPS):
                item = part * GROUPS + group
                if item > tracers:
                    continue
                low = left_t[item] if item < tracers else left_c[...]
                high = right_t[item] if item < tracers else right_c[...]
                moved = jnp.where(
                    from_left,
                    lane_roll(low, EDGE * group),
                    lane_roll(high, EDGE * (group + 1)),
                )
                total = jnp.where(lane // EDGE == group, moved, total)
            out[part * pad : part * pad + levels, :] = total
        top = pl.cdiv(tracers + 1, GROUPS) * pad
        for item in range(tracers):
            out[top + item : top + item + 1, :] = jnp.where(
                from_left, left_t[item, 0:1, :], right_t[item, 0:1, :]
            )
        out[top + tracers : top + tracers + 1, :] = jnp.where(
            from_left, left_c[0:1, :], right_c[0:1, :]
        )


def pack(tracers_t, courant):
    tracers, levels, span = tracers_t.shape
    pad = pl.cdiv(levels, 8) * 8
    rows = pl.cdiv(tracers + 1, GROUPS) * pad + pl.cdiv(tracers + 1, 8) * 8
    message = jax.ShapeDtypeStruct((rows, LANES), f32)
    return pl.pallas_call(
        functools.partial(pack_kernel, tracers, levels),
        out_shape=(message, message),
        in_specs=[HBM, HBM],
        out_specs=(VMEM, VMEM),
        scratch_shapes=[
            pltpu.VMEM((tracers, levels, LANES), f32),
            pltpu.VMEM((tracers, levels, LANES), f32),
            pltpu.VMEM((levels, LANES), f32),
            pltpu.VMEM((levels, LANES), f32),
            pltpu.SemaphoreType.DMA((4,)),
        ],
        compiler_params=params(56 * 1024 * 1024),
        name="pack_edges",
    )(tracers_t, courant)


def prepare_kernel(chunk, dest_ref, row_ref, weights_hbm, _, slot_ref, back_ref, weights, sem):
    copy = pltpu.make_async_copy(weights_hbm, weights, sem)
    copy.start()
    tile, sub, tiles, subs = place()
    count = slot_ref.shape[0]
    mine = pl.ds((tile * subs + sub) * count, count)
    dest = dest_ref[mine, :]
    apart = (dest // subs) ^ tile
    core = (dest % subs + subs - sub) % subs * tiles
    row = row_ref[mine, :]
    slot_ref[...] = (core + apart) * chunk + row
    back_ref[...] = (core + apart % 2 * (tiles // 2) + apart // 2) * chunk + row
    copy.wait()


def prepare(dest, row, weights, after, chunk):
    blocks = weights.shape[0]
    whole = (dest.size // LANES, LANES)
    return pl.pallas_call(
        functools.partial(prepare_kernel, chunk),
        out_shape=(jax.ShapeDtypeStruct((blocks // LANES, LANES), jnp.int32),) * 2
        + (jax.ShapeDtypeStruct(weights.shape, weights.dtype),),
        in_specs=[VMEM, VMEM, HBM, ANY],
        out_specs=(VMEM, VMEM, VMEM),
        scratch_shapes=[pltpu.SemaphoreType.DMA],
        compiler_params=params(44 * 1024 * 1024),
        name="prepare_blocks",
    )(dest.reshape(whole), row.reshape(whole), weights, after)


def high_low(x):
    high = x.astype(bf16)
    return high, (x - high.astype(f32)).astype(bf16)


def forward_kernel(
    dims, slot_ref, patch_ref, level0, courant0, air, msg_a, msg_b, state, weights,
    send_ref, keep_ref, surface, total,
):
    tracers, span, top = dims
    blocks = weights.shape[0]
    even = is_even()
    a, b = msg_a[top : top + tracers + 1, :], msg_b[top : top + tracers + 1, :]
    left, right = jnp.where(even, b, a), jnp.where(even, a, b)
    q = jnp.concatenate([left[:tracers], level0[...], right[:tracers]], axis=1)
    c = jnp.concatenate([left[tracers:], courant0[0:1, :], right[tracers:]], axis=1)
    advected = advect(q, *coefficients(c))[:, LANES : LANES + span]
    fields = jnp.concatenate([advected, air[...]], axis=0).astype(bf16)
    for p in range(span // LANES):
        surface[p] = fields[:, p * LANES : (p + 1) * LANES]
    total[...] = jnp.zeros_like(total)
    zero = jnp.zeros(surface.shape[1:], bf16)
    height = zero.shape[0]

    def step(g, carry):
        base = g * UNROLL
        products = []
        for u in range(0, UNROLL, 2):
            first, second = surface[patch_ref[base + u]], surface[patch_ref[base + u + 1]]
            rows = jnp.concatenate(
                [jnp.concatenate([first, zero], 1), jnp.concatenate([zero, second], 1)], 0
            )
            pair = weights[pl.ds(base + u, 2)].reshape(2 * LANES, LANES)
            both = jnp.dot(rows, pair, preferred_element_type=f32)
            products += [both[:height], both[height:]]
        for u in range(UNROLL):
            total[slot_ref[(base + u) // LANES, (base + u) % LANES]] += products[u]
        return carry

    lax.fori_loop(0, blocks // UNROLL, step, 0)
    half = total.shape[0] // 2
    keep_ref[...] = total[:half]
    send_ref[:half] = total[half:].astype(bf16)
    _, sub, _, subs = place()
    beside = jnp.where(sub == subs - 1, state[0], state[state.shape[0] - 1])
    send_ref[half], send_ref[half + 1] = high_low(beside)


def forward(slot, patch, level0, courant, air, msg_a, msg_b, state, weights, rows):
    tracers, span = level0.shape
    levels = courant.shape[0]
    fields = tracers + air.shape[0]
    pad = pl.cdiv(levels, 8) * 8
    top = pl.cdiv(tracers + 1, GROUPS) * pad
    return pl.pallas_call(
        functools.partial(forward_kernel, (tracers, span, top)),
        out_shape=(
            jax.ShapeDtypeStruct((rows // 2 + 2, fields, LANES), bf16),
            jax.ShapeDtypeStruct((rows // 2, fields, LANES), f32),
        ),
        in_specs=[SMEM] * 2 + [VMEM] * 7,
        out_specs=(VMEM, VMEM),
        scratch_shapes=[
            pltpu.VMEM((span // LANES, fields, LANES), bf16),
            pltpu.VMEM((rows, fields, LANES), f32),
        ],
        compiler_params=params(28 * 1024 * 1024),
        name="blocks_to_rows",
    )(slot, patch, level0, courant, air, msg_a, msg_b, state, weights)


def with_edges(d):
    return d & (d + 1) == 0


def merge_kernel(chunk, keep, got, state, own_ref, beside_ref, *outs):
    rows, fields, lanes = state.shape
    lane = lax.broadcasted_iota(jnp.int32, (fields, lanes), 1)
    edges = jnp.zeros((fields, lanes), f32)
    for r in range(rows):
        edges = jnp.where(lane == r, lane_roll(state[r], r + 1), edges)
        edges = jnp.where(lane == rows + r, lane_roll(state[r], rows + r), edges)
    sign = jnp.where(lax.broadcasted_iota(jnp.int32, (fields, lanes), 0) < fields - 2, 1.0, -1.0)
    mirror = lax.broadcasted_iota(jnp.int32, (lanes, lanes), 0) + lax.broadcasted_iota(
        jnp.int32, (lanes, lanes), 1
    )
    mirror = jnp.where(mirror == lanes - 1, 1.0, 0.0).astype(bf16)
    fold = [
        (jnp.dot(part, mirror, preferred_element_type=f32) * sign).astype(bf16)
        for part in high_low(state[rows - 1])
    ]
    more = [*high_low(edges), *fold]
    own_ref[...] = keep[:chunk] + got[:chunk].astype(f32)
    for d, out in enumerate(outs, 1):
        part = slice(d * chunk, (d + 1) * chunk)
        out[:chunk] = (keep[part] + got[part].astype(f32)).astype(bf16)
        if with_edges(d):
            for i, extra in enumerate(more):
                out[chunk + i] = extra
    last = keep.shape[0]
    beside_ref[...] = got[last].astype(f32) + got[last + 1].astype(f32)


def merge(keep, got, state, chunk):
    rows, fields, lanes = keep.shape
    count = rows // chunk
    return pl.pallas_call(
        functools.partial(merge_kernel, chunk),
        out_shape=(
            jax.ShapeDtypeStruct((chunk, fields, lanes), f32),
            jax.ShapeDtypeStruct((fields, lanes), f32),
        )
        + tuple(
            jax.ShapeDtypeStruct((chunk + 4 * with_edges(d), fields, lanes), bf16)
            for d in range(1, count)
        ),
        in_specs=[VMEM] * 3,
        out_specs=(VMEM,) * (count + 1),
        compiler_params=params((10 if count < 16 else 24) * 1024 * 1024),
        name="merge_cores",
    )(keep, got, state)


def ocean_kernel(count, state, beside, rate, wet, own, *rest):
    got, (next_ref, half_ref) = rest[:count], rest[-2:]
    rows, fields, lanes = state.shape
    lane = lax.broadcasted_iota(jnp.int32, (fields, lanes), 1)
    tile, sub, tiles, subs = place()
    to_east, to_west = tile ^ ((tile + 1) % tiles), tile ^ ((tile + tiles - 1) % tiles)

    def extra(chunk, i):
        return chunk[rows + i].astype(f32) + chunk[rows + i + 1].astype(f32)

    from_east = from_west = jnp.zeros((fields, lanes), f32)
    for d, chunk in enumerate(got, 1):
        if with_edges(d):
            edges = extra(chunk, 0)
            from_east = jnp.where(to_east == d, edges, from_east)
            from_west = jnp.where(to_west == d, edges, from_west)
    south = jnp.where(sub == 0, 0.0, beside[...])
    north = jnp.where(sub == subs - 1, extra(got[-1], 2), beside[...])
    for r in range(rows):
        here = state[r]
        west = jnp.where(lane == 0, lane_roll(from_west, -r), lane_roll(here, 1))
        east = jnp.where(
            lane == lanes - 1, lane_roll(from_east, lanes - 1 - rows - r), lane_roll(here, -1)
        )
        below = state[r - 1] if r else south
        above = state[r + 1] if r < rows - 1 else north
        lateral = west + east + below + above - 4.0 * here
        remapped = own[r]
        for chunk in got:
            remapped = remapped + chunk[r].astype(f32)
        new = here + wet[r : r + 1, :].astype(f32) * (
            rate[r : r + 1, :] * (remapped - here) + NU * lateral
        )
        next_ref[r] = new
        half_ref[r] = new.astype(bf16)


def ocean(state, beside, rate, wet, own, got, after):
    rows, fields, lanes = state.shape
    return pl.pallas_call(
        functools.partial(ocean_kernel, len(got)),
        out_shape=(
            jax.ShapeDtypeStruct(state.shape, f32),
            jax.ShapeDtypeStruct(state.shape, bf16),
        ),
        in_specs=[VMEM] * (5 + len(got)) + [ANY],
        out_specs=(VMEM, VMEM),
        compiler_params=params(8 * 1024 * 1024),
        name="ocean_update",
    )(state, beside, rate, wet, own, *got, after)


def gather_kernel(count, *refs):
    out = refs[-1]
    chunk = refs[0].shape[0]
    for i in range(count):
        out[i * chunk : (i + 1) * chunk] = refs[i][...]


def gather_rows(parts, *after):
    chunk, fields, lanes = parts[0].shape
    return pl.pallas_call(
        functools.partial(gather_kernel, len(parts)),
        out_shape=jax.ShapeDtypeStruct((chunk * len(parts), fields, lanes), bf16),
        in_specs=[VMEM] * len(parts) + [ANY] * len(after),
        out_specs=VMEM,
        compiler_params=params(8 * 1024 * 1024),
        name="gather_rows",
    )(*parts, *after)


def advect_kernel(
    tracers, levels, first, group, q_ref, c_ref, msg_a, msg_b, *rest
):
    out_ref, flag_ref, right, left, own, band, *scratch = rest[-6 - 2 * SETS :]
    even = is_even()
    span = q_ref.shape[2]
    pad = pl.cdiv(levels, 8) * 8
    tiles = span // LANES + 2
    tile = lambda i: slice(i * LANES, (i + 1) * LANES)

    def sides(item):
        start = pl.multiple_of(item // GROUPS * pad, 8)
        shift = EDGE * (item % GROUPS)
        a, b = msg_a[pl.ds(start, levels), :], msg_b[pl.ds(start, levels), :]
        before, after = jnp.where(even, b, a), jnp.where(even, a, b)
        return (
            pltpu.roll(before, (2 * LANES - EDGE - shift) % LANES, 1),
            pltpu.roll(after, (LANES - shift) % LANES, 1),
        )

    @pl.when(pl.program_id(0) == 0)
    def _():
        before, after = sides(tracers)
        c = jnp.concatenate([before, c_ref[...], after], axis=1)
        for ref, value in zip((right, left, own), coefficients(c)):
            ref[...] = jnp.zeros_like(ref)
            for i in range(tiles):
                ref[i, :levels] = value[:, tile(i)]
        for state in scratch[:SETS]:
            state[...] = jnp.zeros_like(state)
        r = lax.broadcasted_iota(jnp.int32, band.shape, 0) % (2 * LANES)
        j = lax.broadcasted_iota(jnp.int32, band.shape, 1)
        column = jnp.where(r < LANES, r, jnp.where(r < LANES + LANES // 2, r, r - 2 * LANES))
        d = column - jnp.where(j < LANES, j, j - LANES - 1)
        weight = jnp.where((d == 0) | (d == 1), 7.0, jnp.where((d == -1) | (d == 2), -1.0, 0.0))
        band[...] = weight.astype(bf16)
        flag_ref[...] = jnp.zeros_like(flag_ref)

    sets = SETS
    states, operands = scratch[:sets], scratch[sets:]
    each = group // sets
    for t in range(group):
        state, at = states[t // each], t % each
        before, after = sides(pl.program_id(0) * group + first + t)
        part = slice(at * pad, at * pad + levels)
        state[0, part] = before
        for i in range(1, tiles - 1):
            state[i, part] = q_ref[t, :, tile(i - 1)]
        state[tiles - 1, part] = after

    rows = each * pad
    lane = lax.broadcasted_iota(jnp.int32, (rows, LANES), 1)

    def edge_values(state, lhs):
        halves = [high_low(state[i]) for i in range(tiles)]
        for i in range(tiles):
            part = slice(i * rows, (i + 1) * rows)
            for h in range(2):
                lhs[part, tile(2 * h)] = halves[i][h]
                lhs[part, tile(2 * h + 1)] = jnp.where(
                    lane < LANES // 2, halves[min(i + 1, tiles - 1)][h], halves[max(i - 1, 0)][h]
                )
        return jnp.dot(lhs[...], band[...], preferred_element_type=f32)

    def advance(state, edges):
        last = None
        for i in range(tiles):
            edge = edges[i * rows : (i + 1) * rows].reshape(each, pad, 2 * LANES)
            q = state[i]
            flux = (
                right[i] * edge[..., :LANES]
                - left[i] * edge[..., LANES:]
                + own[i] * q.reshape(each, pad, LANES)
            ).reshape(rows, LANES)
            moved = pltpu.roll(flux, 1, 1)
            before = moved if last is None else jnp.where(lane == 0, last, moved)
            state[i] = q - (flux - before)
            last = moved

    pending = None
    for step in range(ASTEPS):
        for k in range(sets):
            edges = edge_values(states[k], operands[k])
            if pending is not None:
                advance(*pending)
            pending = (states[k], edges)
    advance(*pending)

    for t in range(group):
        for i in range(1, tiles - 1):
            at = t % each * pad
            out_ref[t, :, tile(i - 1)] = states[t // each][i, at : at + levels]


def advect_some(tracers_t, courant, msg_a, msg_b, first, count, after, into=None):
    tracers, levels, span = tracers_t.shape
    group = GROUP
    tiles, pad = span // LANES + 2, pl.cdiv(levels, 8) * 8
    whole = lambda shape: pl.BlockSpec(shape, lambda i: (0,) * len(shape))
    block = pl.BlockSpec((group, levels, span), lambda i: (i + first // group, 0, 0))
    more = [after] if into is None else [after, into]
    return pl.pallas_call(
        functools.partial(advect_kernel, tracers, levels, first, group),
        grid=(count // group,),
        out_shape=(
            jax.ShapeDtypeStruct(tracers_t.shape, f32),
            jax.ShapeDtypeStruct((8, LANES), f32),
        ),
        in_specs=[
            block,
            whole(courant.shape),
            whole(msg_a.shape),
            whole(msg_b.shape),
        ]
        + [ANY] * len(more),
        out_specs=(block, whole((8, LANES))),
        input_output_aliases={} if into is None else {5: 0},
        scratch_shapes=[pltpu.VMEM((tiles, pad, LANES), f32)] * 3
        + [pltpu.VMEM((4 * LANES, 2 * LANES), bf16)]
        + [pltpu.VMEM((tiles, group // SETS * pad, LANES), f32)] * SETS
        + [pltpu.VMEM((tiles * group // SETS * pad, 4 * LANES), bf16)] * SETS,
        compiler_params=params(12 * 1024 * 1024),
        cost_estimate=pl.CostEstimate(
            flops=200 * count * levels * span,
            bytes_accessed=8 * count * levels * span,
            transcendentals=0,
        ),
        name="advect_levels",
    )(tracers_t, courant, msg_a, msg_b, *more)


def backward_kernel(
    slot_ref, patch_ref, even, odd, even_other, odd_other, weights, advected_hbm, air_hbm, out_hbm,
    rows, total, bottom, air, sem, air_sem,
):
    fetch = pltpu.make_async_copy(advected_hbm.at[:, pl.ds(0, 8), :], bottom, sem)
    fetch.start()
    tracers, _, span = bottom.shape
    blocks = weights.shape[0]
    part, fields, _ = even.shape
    for i, some in enumerate((even, odd, even_other, odd_other)):
        rows[i * part : (i + 1) * part] = some[...]
    total[...] = jnp.zeros_like(total)
    slot_of = lambda b: slot_ref[b // LANES, b % LANES]

    def step(g, carry):
        base = g * UNROLL
        products = []
        for u in range(0, UNROLL, 2):
            both = lax.dot_general(
                jnp.concatenate([rows[slot_of(base + u)], rows[slot_of(base + u + 1)]], 0),
                weights[pl.ds(base + u, 2)].reshape(2 * LANES, LANES),
                (((1,), (1,)), ((), ())),
                preferred_element_type=f32,
            )
            products += [both[:fields, :LANES], both[fields:, LANES:]]
        for u in range(UNROLL):
            total[patch_ref[base + u]] += products[u]
        return carry

    lax.fori_loop(0, blocks // UNROLL, step, 0)
    fetch.wait()
    for p in range(span // LANES):
        part = slice(p * LANES, (p + 1) * LANES)
        exchange = total[p]
        air[:, part] = exchange
        bottom[:, 0, part] += COUPLE * exchange[:tracers]
    stores = (
        pltpu.make_async_copy(bottom, out_hbm.at[:, pl.ds(0, 8), :], sem),
        pltpu.make_async_copy(air, air_hbm, air_sem),
    )
    for store in stores:
        store.start()
    for store in stores:
        store.wait()


def backward(slot, patch, parts, weights, advected):
    tracers, levels, span = advected.shape
    part, fields, lanes = parts[0].shape
    return pl.pallas_call(
        backward_kernel,
        out_shape=(
            jax.ShapeDtypeStruct((fields, span), f32),
            jax.ShapeDtypeStruct(advected.shape, f32),
        ),
        in_specs=[SMEM, SMEM] + [VMEM] * 5 + [HBM],
        out_specs=(HBM, HBM),
        input_output_aliases={7: 1},
        scratch_shapes=[
            pltpu.VMEM((4 * part, fields, lanes), bf16),
            pltpu.VMEM((span // lanes, fields, lanes), f32),
            pltpu.VMEM((tracers, 8, span), f32),
            pltpu.VMEM((fields, span), f32),
            pltpu.SemaphoreType.DMA,
            pltpu.SemaphoreType.DMA,
        ],
        compiler_params=params(16 * 1024 * 1024),
        name="rows_to_columns",
    )(slot, patch, *parts, weights, advected)


def per_device(
    tracers,
    courant,
    air_surface,
    block_weights,
    block_dest,
    block_row,
    block_patch,
    ocean_state,
    exchange_rate,
    sea_mask,
):
    tiles, subs = lax.axis_size("tile"), lax.axis_size("sub")
    devices = tiles * subs
    ocean_rows = ocean_state.shape[1]
    flat = ("tile", "sub")
    tracers_t = jnp.transpose(tracers, (1, 0, 2))
    pack_a, pack_b = pack(tracers_t, courant)
    msg_b = lax.ppermute(
        pack_b, flat, [(i, (i + 1 if i % 2 else i - 1) % devices) for i in range(devices)]
    )
    msg_a = lax.ppermute(pack_a, flat, [(i, i ^ 1) for i in range(devices)])

    slot, slot_back, weights = prepare(
        block_dest, block_row, block_weights, pack_b, ocean_rows
    )
    state = jnp.transpose(ocean_state, (1, 0, 2))
    send, keep = forward(
        slot, block_patch, tracers[0], courant, air_surface, msg_a, msg_b, state,
        weights, devices * ocean_rows,
    )
    swap = [(0, 1), (1, 0)]
    got = lax.ppermute(send, "sub", swap)
    own, beside, *partial = merge(keep, got, state, ocean_rows)
    across = lambda x, d: lax.ppermute(x, "tile", [(i, i ^ d) for i in range(tiles)])
    got = [across(x, d) for d, x in enumerate(partial, 1)]

    advance = functools.partial(advect_some, tracers_t, courant, msg_a, msg_b)
    count = tracers.shape[1] // 3
    some, flag = advance(0, count, own)
    next_ocean, half = ocean(
        state, beside, exchange_rate, sea_mask, own, got, flag
    )

    arrived = [across(half, d) for d in range(tiles - 2, 0, -2)]
    some, flag = advance(count, count, half, some)
    even = gather_rows([half] + arrived[::-1], flag)
    odd = across(even, 1)
    even_other = lax.ppermute(even, "sub", swap)
    advected, flag = advance(2 * count, tracers.shape[1] - 2 * count, even, some)
    odd = gather_rows([odd], flag)
    odd_other = lax.ppermute(odd, "sub", swap)
    air_exchange, out_t = backward(
        slot_back, block_patch, (even, odd, even_other, odd_other), weights, advected
    )
    return jnp.transpose(out_t, (1, 0, 2)), jnp.transpose(next_ocean, (1, 0, 2)), air_exchange


def solution(mesh):
    placed = (
        P("members", None, ("tile", "sub")),
        P("members", ("tile", "sub")),
        P("members", ("tile", "sub")),
        P(("tile", "sub"), None, None),
        P(),
        P(),
        P(("tile", "sub")),
        P("members", "sub", "tile"),
        P("sub", "tile"),
        P("sub", "tile"),
    )
    return jax.shard_map(
        per_device,
        mesh=mesh,
        in_specs=placed,
        out_specs=(
            P("members", None, ("tile", "sub")),
            P("members", "sub", "tile"),
            P("members", ("tile", "sub")),
        ),
        check_vma=False,
    )
```

```python
import functools

import jax
import jax.numpy as jnp
from jax import lax
from jax.experimental import pallas as pl
from jax.experimental.pallas import tpu as pltpu
from jax.sharding import PartitionSpec as P

ASTEPS = 3
NU = 0.2
COUPLE = 0.5
LANES = 128
EDGE = 16
GROUPS = LANES // EDGE
UNROLL = 128
GROUP = 4
SETS = 2

VMEM = pl.BlockSpec(memory_space=pltpu.VMEM)
SMEM = pl.BlockSpec(memory_space=pltpu.SMEM)
ANY = pl.BlockSpec(memory_space=pl.ANY)
HBM = pl.BlockSpec(memory_space=pltpu.HBM)
f32 = jnp.float32
bf16 = jnp.bfloat16


def params(limit):
    return pltpu.CompilerParams(vmem_limit_bytes=limit)


def place():
    sizes = lax.axis_size("tile"), lax.axis_size("sub")
    return lax.axis_index("tile"), lax.axis_index("sub"), *sizes


def pass_kernel(x_ref, out_ref):
    out_ref[...] = x_ref[...]


def pass_on(x):
    return pl.pallas_call(
        pass_kernel,
        out_shape=jax.ShapeDtypeStruct(x.shape, x.dtype),
        in_specs=[VMEM],
        out_specs=VMEM,
        compiler_params=params(2 * 1024 * 1024),
        name="pass_on",
    )(x)


def is_even():
    tile, sub, _, subs = place()
    return (tile * subs + sub) % 2 == 0


def lane_roll(x, shift):
    length = x.shape[-1]
    shift = shift % length
    return x if shift == 0 else pltpu.roll(x, shift, x.ndim - 1)


def coefficients(c):
    d = 1.0 - c
    return c * d * d * (1.0 / 12.0), c * c * d * (1.0 / 12.0), c * c * (3.0 - 2.0 * c)


def advect(q, right, left, own):
    for _ in range(ASTEPS):
        pair = q + lane_roll(q, -1)
        edge = 8.0 * pair - (lane_roll(pair, 1) + lane_roll(pair, -1))
        flux = right * edge - left * lane_roll(edge, 1) + own * q
        q = q - (flux - lane_roll(flux, 1))
    return q


def pack_kernel(
    tracers, levels, q_hbm, c_hbm, a_ref, b_ref, left_t, right_t, left_c, right_c, sems
):
    span = q_hbm.shape[2]
    copies = [
        pltpu.make_async_copy(src, dst, sems.at[i])
        for i, (src, dst) in enumerate(
            (
                (q_hbm.at[:, :, pl.ds(0, LANES)], left_t),
                (q_hbm.at[:, :, pl.ds(span - LANES, LANES)], right_t),
                (c_hbm.at[:, pl.ds(0, LANES)], left_c),
                (c_hbm.at[:, pl.ds(span - LANES, LANES)], right_c),
            )
        )
    ]
    for copy in copies:
        copy.start()
    for copy in copies:
        copy.wait()
    even = is_even()
    lane = lax.broadcasted_iota(jnp.int32, (levels, LANES), 1)
    pad = pl.cdiv(levels, 8) * 8
    for out, from_left in ((a_ref, jnp.logical_not(even)), (b_ref, even)):
        for part in range(pl.cdiv(tracers + 1, GROUPS)):
            total = jnp.zeros((levels, LANES), f32)
            for group in range(GROUPS):
                item = part * GROUPS + group
                if item > tracers:
                    continue
                low = left_t[item] if item < tracers else left_c[...]
                high = right_t[item] if item < tracers else right_c[...]
                moved = jnp.where(
                    from_left,
                    lane_roll(low, EDGE * group),
                    lane_roll(high, EDGE * (group + 1)),
                )
                total = jnp.where(lane // EDGE == group, moved, total)
            out[part * pad : part * pad + levels, :] = total
        top = pl.cdiv(tracers + 1, GROUPS) * pad
        for item in range(tracers):
            out[top + item : top + item + 1, :] = jnp.where(
                from_left, left_t[item, 0:1, :], right_t[item, 0:1, :]
            )
        out[top + tracers : top + tracers + 1, :] = jnp.where(
            from_left, left_c[0:1, :], right_c[0:1, :]
        )


def pack(tracers_t, courant):
    tracers, levels, span = tracers_t.shape
    pad = pl.cdiv(levels, 8) * 8
    rows = pl.cdiv(tracers + 1, GROUPS) * pad + pl.cdiv(tracers + 1, 8) * 8
    message = jax.ShapeDtypeStruct((rows, LANES), f32)
    return pl.pallas_call(
        functools.partial(pack_kernel, tracers, levels),
        out_shape=(message, message),
        in_specs=[HBM, HBM],
        out_specs=(VMEM, VMEM),
        scratch_shapes=[
            pltpu.VMEM((tracers, levels, LANES), f32),
            pltpu.VMEM((tracers, levels, LANES), f32),
            pltpu.VMEM((levels, LANES), f32),
            pltpu.VMEM((levels, LANES), f32),
            pltpu.SemaphoreType.DMA((4,)),
        ],
        compiler_params=params(56 * 1024 * 1024),
        name="pack_edges",
    )(tracers_t, courant)


def prepare_kernel(chunk, dest_ref, row_ref, weights_hbm, slot_ref, back_ref, weights, sem):
    copy = pltpu.make_async_copy(weights_hbm, weights, sem)
    copy.start()
    tile, sub, tiles, subs = place()
    count = slot_ref.shape[0]
    mine = pl.ds((tile * subs + sub) * count, count)
    dest = dest_ref[mine, :]
    apart = (dest // subs) ^ tile
    core = (dest % subs + subs - sub) % subs * tiles
    row = row_ref[mine, :]
    slot_ref[...] = (core + apart) * chunk + row
    far = tiles // 2
    back = jnp.where(apart < far, apart, far + apart % 2 * (far // 2) + (apart - far) // 2)
    back_ref[...] = (core + back) * chunk + row
    copy.wait()


def prepare(dest, row, weights, chunk):
    blocks = weights.shape[0]
    whole = (dest.size // LANES, LANES)
    return pl.pallas_call(
        functools.partial(prepare_kernel, chunk),
        out_shape=(jax.ShapeDtypeStruct((blocks // LANES, LANES), jnp.int32),) * 2
        + (jax.ShapeDtypeStruct(weights.shape, weights.dtype),),
        in_specs=[VMEM, VMEM, HBM],
        out_specs=(VMEM, VMEM, VMEM),
        scratch_shapes=[pltpu.SemaphoreType.DMA],
        compiler_params=params(44 * 1024 * 1024),
        name="prepare_blocks",
    )(dest.reshape(whole), row.reshape(whole), weights)


def high_low(x):
    high = x.astype(bf16)
    return high, (x - high.astype(f32)).astype(bf16)


def forward_kernel(
    dims, slot_ref, patch_ref, level0, courant0, air, msg_a, msg_b, state, weights,
    send_ref, keep_ref, surface, total,
):
    tracers, span, top = dims
    blocks = weights.shape[0]
    even = is_even()
    a, b = msg_a[top : top + tracers + 1, :], msg_b[top : top + tracers + 1, :]
    left, right = jnp.where(even, b, a), jnp.where(even, a, b)
    q = jnp.concatenate([left[:tracers], level0[...], right[:tracers]], axis=1)
    c = jnp.concatenate([left[tracers:], courant0[0:1, :], right[tracers:]], axis=1)
    advected = advect(q, *coefficients(c))[:, LANES : LANES + span]
    fields = jnp.concatenate([advected, air[...]], axis=0).astype(bf16)
    for p in range(span // LANES):
        surface[p] = fields[:, p * LANES : (p + 1) * LANES]
    total[...] = jnp.zeros_like(total)
    zero = jnp.zeros(surface.shape[1:], bf16)
    height = zero.shape[0]

    def step(g, carry):
        base = g * UNROLL
        products = []
        for u in range(0, UNROLL, 2):
            first, second = surface[patch_ref[base + u]], surface[patch_ref[base + u + 1]]
            rows = jnp.concatenate(
                [jnp.concatenate([first, zero], 1), jnp.concatenate([zero, second], 1)], 0
            )
            pair = weights[pl.ds(base + u, 2)].reshape(2 * LANES, LANES)
            both = jnp.dot(rows, pair, preferred_element_type=f32)
            products += [both[:height], both[height:]]
        for u in range(UNROLL):
            total[slot_ref[(base + u) // LANES, (base + u) % LANES]] += products[u]
        return carry

    lax.fori_loop(0, blocks // UNROLL, step, 0)
    half = total.shape[0] // 2
    keep_ref[...] = total[:half]
    send_ref[:half] = total[half:].astype(bf16)
    _, sub, _, subs = place()
    beside = jnp.where(sub == subs - 1, state[0], state[state.shape[0] - 1])
    send_ref[half], send_ref[half + 1] = high_low(beside)


def forward(slot, patch, level0, courant, air, msg_a, msg_b, state, weights, rows):
    tracers, span = level0.shape
    levels = courant.shape[0]
    fields = tracers + air.shape[0]
    pad = pl.cdiv(levels, 8) * 8
    top = pl.cdiv(tracers + 1, GROUPS) * pad
    return pl.pallas_call(
        functools.partial(forward_kernel, (tracers, span, top)),
        out_shape=(
            jax.ShapeDtypeStruct((rows // 2 + 2, fields, LANES), bf16),
            jax.ShapeDtypeStruct((rows // 2, fields, LANES), f32),
        ),
        in_specs=[SMEM] * 2 + [VMEM] * 7,
        out_specs=(VMEM, VMEM),
        scratch_shapes=[
            pltpu.VMEM((span // LANES, fields, LANES), bf16),
            pltpu.VMEM((rows, fields, LANES), f32),
        ],
        compiler_params=params(28 * 1024 * 1024),
        name="blocks_to_rows",
    )(slot, patch, level0, courant, air, msg_a, msg_b, state, weights)


def with_edges(d):
    return d & (d + 1) == 0


def merge_kernel(chunk, keep, got, state, own_ref, beside_ref, *outs):
    rows, fields, lanes = state.shape
    lane = lax.broadcasted_iota(jnp.int32, (fields, lanes), 1)
    edges = jnp.zeros((fields, lanes), f32)
    for r in range(rows):
        edges = jnp.where(lane == r, lane_roll(state[r], r + 1), edges)
        edges = jnp.where(lane == rows + r, lane_roll(state[r], rows + r), edges)
    sign = jnp.where(lax.broadcasted_iota(jnp.int32, (fields, lanes), 0) < fields - 2, 1.0, -1.0)
    mirror = lax.broadcasted_iota(jnp.int32, (lanes, lanes), 0) + lax.broadcasted_iota(
        jnp.int32, (lanes, lanes), 1
    )
    mirror = jnp.where(mirror == lanes - 1, 1.0, 0.0).astype(bf16)
    fold = [
        (jnp.dot(part, mirror, preferred_element_type=f32) * sign).astype(bf16)
        for part in high_low(state[rows - 1])
    ]
    more = [*high_low(edges), *fold]
    own_ref[...] = keep[:chunk] + got[:chunk].astype(f32)
    for d, out in enumerate(outs, 1):
        part = slice(d * chunk, (d + 1) * chunk)
        out[:chunk] = (keep[part] + got[part].astype(f32)).astype(bf16)
        if with_edges(d):
            for i, extra in enumerate(more):
                out[chunk + i] = extra
    last = keep.shape[0]
    beside_ref[...] = got[last].astype(f32) + got[last + 1].astype(f32)


def merge(keep, got, state, chunk):
    rows, fields, lanes = keep.shape
    count = rows // chunk
    return pl.pallas_call(
        functools.partial(merge_kernel, chunk),
        out_shape=(
            jax.ShapeDtypeStruct((chunk, fields, lanes), f32),
            jax.ShapeDtypeStruct((fields, lanes), f32),
        )
        + tuple(
            jax.ShapeDtypeStruct((chunk + 4 * with_edges(d), fields, lanes), bf16)
            for d in range(1, count)
        ),
        in_specs=[VMEM] * 3,
        out_specs=(VMEM,) * (count + 1),
        compiler_params=params((10 if count < 16 else 24) * 1024 * 1024),
        name="merge_cores",
    )(keep, got, state)


def ocean_kernel(count, state, beside, rate, wet, own, *rest):
    got, (next_ref, half_ref) = rest[:count], rest[-2:]
    rows, fields, lanes = state.shape
    lane = lax.broadcasted_iota(jnp.int32, (fields, lanes), 1)
    tile, sub, tiles, subs = place()
    to_east, to_west = tile ^ ((tile + 1) % tiles), tile ^ ((tile + tiles - 1) % tiles)

    def extra(chunk, i):
        return chunk[rows + i].astype(f32) + chunk[rows + i + 1].astype(f32)

    from_east = from_west = jnp.zeros((fields, lanes), f32)
    for d, chunk in enumerate(got, 1):
        if with_edges(d):
            edges = extra(chunk, 0)
            from_east = jnp.where(to_east == d, edges, from_east)
            from_west = jnp.where(to_west == d, edges, from_west)
    south = jnp.where(sub == 0, 0.0, beside[...])
    north = jnp.where(sub == subs - 1, extra(got[-1], 2), beside[...])
    for r in range(rows):
        here = state[r]
        west = jnp.where(lane == 0, lane_roll(from_west, -r), lane_roll(here, 1))
        east = jnp.where(
            lane == lanes - 1, lane_roll(from_east, lanes - 1 - rows - r), lane_roll(here, -1)
        )
        below = state[r - 1] if r else south
        above = state[r + 1] if r < rows - 1 else north
        lateral = west + east + below + above - 4.0 * here
        remapped = own[r]
        for chunk in got:
            remapped = remapped + chunk[r].astype(f32)
        new = here + wet[r : r + 1, :].astype(f32) * (
            rate[r : r + 1, :] * (remapped - here) + NU * lateral
        )
        next_ref[r] = new
        half_ref[r] = new.astype(bf16)


def ocean(state, beside, rate, wet, own, got, after):
    rows, fields, lanes = state.shape
    return pl.pallas_call(
        functools.partial(ocean_kernel, len(got)),
        out_shape=(
            jax.ShapeDtypeStruct(state.shape, f32),
            jax.ShapeDtypeStruct(state.shape, bf16),
        ),
        in_specs=[VMEM] * (5 + len(got)) + [ANY],
        out_specs=(VMEM, VMEM),
        compiler_params=params(8 * 1024 * 1024),
        name="ocean_update",
    )(state, beside, rate, wet, own, *got, after)


def gather_kernel(count, *refs):
    out, start = refs[-1], 0
    for ref in refs[:count]:
        out[start : start + ref.shape[0]] = ref[...]
        start += ref.shape[0]


def gather_rows(parts, *after):
    fields, lanes = parts[0].shape[1:]
    rows = sum(part.shape[0] for part in parts)
    return pl.pallas_call(
        functools.partial(gather_kernel, len(parts)),
        out_shape=jax.ShapeDtypeStruct((rows, fields, lanes), bf16),
        in_specs=[VMEM] * len(parts) + [ANY] * len(after),
        out_specs=VMEM,
        compiler_params=params(8 * 1024 * 1024),
        name="gather_rows",
    )(*parts, *after)


def advect_kernel(
    tracers, levels, first, group, q_ref, c_ref, msg_a, msg_b, *rest
):
    out_ref, flag_ref, right, left, own, band, *scratch = rest[-6 - 2 * SETS :]
    even = is_even()
    span = q_ref.shape[2]
    pad = pl.cdiv(levels, 8) * 8
    tiles = span // LANES + 2
    tile = lambda i: slice(i * LANES, (i + 1) * LANES)

    def sides(item):
        start = pl.multiple_of(item // GROUPS * pad, 8)
        shift = EDGE * (item % GROUPS)
        a, b = msg_a[pl.ds(start, levels), :], msg_b[pl.ds(start, levels), :]
        before, after = jnp.where(even, b, a), jnp.where(even, a, b)
        return (
            pltpu.roll(before, (2 * LANES - EDGE - shift) % LANES, 1),
            pltpu.roll(after, (LANES - shift) % LANES, 1),
        )

    @pl.when(pl.program_id(0) == 0)
    def _():
        before, after = sides(tracers)
        c = jnp.concatenate([before, c_ref[...], after], axis=1)
        for ref, value in zip((right, left, own), coefficients(c)):
            ref[...] = jnp.zeros_like(ref)
            for i in range(tiles):
                ref[i, :levels] = value[:, tile(i)]
        for state in scratch[:SETS]:
            state[...] = jnp.zeros_like(state)
        r = lax.broadcasted_iota(jnp.int32, band.shape, 0) % (2 * LANES)
        j = lax.broadcasted_iota(jnp.int32, band.shape, 1)
        column = jnp.where(r < LANES, r, jnp.where(r < LANES + LANES // 2, r, r - 2 * LANES))
        d = column - jnp.where(j < LANES, j, j - LANES - 1)
        weight = jnp.where((d == 0) | (d == 1), 7.0, jnp.where((d == -1) | (d == 2), -1.0, 0.0))
        band[...] = weight.astype(bf16)
        flag_ref[...] = jnp.zeros_like(flag_ref)

    sets = SETS
    states, operands = scratch[:sets], scratch[sets:]
    each = group // sets
    for t in range(group):
        state, at = states[t // each], t % each
        before, after = sides(pl.program_id(0) * group + first + t)
        part = slice(at * pad, at * pad + levels)
        state[0, part] = before
        for i in range(1, tiles - 1):
            state[i, part] = q_ref[t, :, tile(i - 1)]
        state[tiles - 1, part] = after

    rows = each * pad
    lane = lax.broadcasted_iota(jnp.int32, (rows, LANES), 1)

    def edge_values(state, lhs):
        halves = [high_low(state[i]) for i in range(tiles)]
        for i in range(tiles):
            part = slice(i * rows, (i + 1) * rows)
            for h in range(2):
                lhs[part, tile(2 * h)] = halves[i][h]
                lhs[part, tile(2 * h + 1)] = jnp.where(
                    lane < LANES // 2, halves[min(i + 1, tiles - 1)][h], halves[max(i - 1, 0)][h]
                )
        return jnp.dot(lhs[...], band[...], preferred_element_type=f32)

    def advance(state, edges):
        last = None
        for i in range(tiles):
            edge = edges[i * rows : (i + 1) * rows].reshape(each, pad, 2 * LANES)
            q = state[i]
            flux = (
                right[i] * edge[..., :LANES]
                - left[i] * edge[..., LANES:]
                + own[i] * q.reshape(each, pad, LANES)
            ).reshape(rows, LANES)
            moved = pltpu.roll(flux, 1, 1)
            before = moved if last is None else jnp.where(lane == 0, last, moved)
            state[i] = q - (flux - before)
            last = moved

    pending = None
    for step in range(ASTEPS):
        for k in range(sets):
            edges = edge_values(states[k], operands[k])
            if pending is not None:
                advance(*pending)
            pending = (states[k], edges)
    advance(*pending)

    for t in range(group):
        for i in range(1, tiles - 1):
            at = t % each * pad
            out_ref[t, :, tile(i - 1)] = states[t // each][i, at : at + levels]


def advect_some(tracers_t, courant, msg_a, msg_b, first, count, after, into=None):
    tracers, levels, span = tracers_t.shape
    group = GROUP
    tiles, pad = span // LANES + 2, pl.cdiv(levels, 8) * 8
    whole = lambda shape: pl.BlockSpec(shape, lambda i: (0,) * len(shape))
    block = pl.BlockSpec((group, levels, span), lambda i: (i + first // group, 0, 0))
    more = [after] if into is None else [after, into]
    return pl.pallas_call(
        functools.partial(advect_kernel, tracers, levels, first, group),
        grid=(count // group,),
        out_shape=(
            jax.ShapeDtypeStruct(tracers_t.shape, f32),
            jax.ShapeDtypeStruct((8, LANES), f32),
        ),
        in_specs=[
            block,
            whole(courant.shape),
            whole(msg_a.shape),
            whole(msg_b.shape),
        ]
        + [ANY] * len(more),
        out_specs=(block, whole((8, LANES))),
        input_output_aliases={} if into is None else {5: 0},
        scratch_shapes=[pltpu.VMEM((tiles, pad, LANES), f32)] * 3
        + [pltpu.VMEM((4 * LANES, 2 * LANES), bf16)]
        + [pltpu.VMEM((tiles, group // SETS * pad, LANES), f32)] * SETS
        + [pltpu.VMEM((tiles * group // SETS * pad, 4 * LANES), bf16)] * SETS,
        compiler_params=params(12 * 1024 * 1024),
        cost_estimate=pl.CostEstimate(
            flops=200 * count * levels * span,
            bytes_accessed=8 * count * levels * span,
            transcendentals=0,
        ),
        name="advect_levels",
    )(tracers_t, courant, msg_a, msg_b, *more)


def backward_kernel(
    slot_ref, patch_ref, mine, odd, other, other_odd, weights, advected_hbm, air_hbm, out_hbm,
    rows, total, bottom, air, sem, air_sem,
):
    fetch = pltpu.make_async_copy(advected_hbm.at[:, pl.ds(0, 8), :], bottom, sem)
    fetch.start()
    tracers, _, span = bottom.shape
    blocks = weights.shape[0]
    fields = mine.shape[1]
    start = 0
    for some in (mine, odd, other, other_odd):
        rows[start : start + some.shape[0]] = some[...]
        start += some.shape[0]
    total[...] = jnp.zeros_like(total)
    slot_of = lambda b: slot_ref[b // LANES, b % LANES]

    def step(g, carry):
        base = g * UNROLL
        products = []
        for u in range(0, UNROLL, 2):
            both = lax.dot_general(
                jnp.concatenate([rows[slot_of(base + u)], rows[slot_of(base + u + 1)]], 0),
                weights[pl.ds(base + u, 2)].reshape(2 * LANES, LANES),
                (((1,), (1,)), ((), ())),
                preferred_element_type=f32,
            )
            products += [both[:fields, :LANES], both[fields:, LANES:]]
        for u in range(UNROLL):
            total[patch_ref[base + u]] += products[u]
        return carry

    lax.fori_loop(0, blocks // UNROLL, step, 0)
    fetch.wait()
    for p in range(span // LANES):
        part = slice(p * LANES, (p + 1) * LANES)
        exchange = total[p]
        air[:, part] = exchange
        bottom[:, 0, part] += COUPLE * exchange[:tracers]
    stores = (
        pltpu.make_async_copy(bottom, out_hbm.at[:, pl.ds(0, 8), :], sem),
        pltpu.make_async_copy(air, air_hbm, air_sem),
    )
    for store in stores:
        store.start()
    for store in stores:
        store.wait()


def backward(slot, patch, parts, weights, advected):
    tracers, levels, span = advected.shape
    fields, lanes = parts[0].shape[1:]
    return pl.pallas_call(
        backward_kernel,
        out_shape=(
            jax.ShapeDtypeStruct((fields, span), f32),
            jax.ShapeDtypeStruct(advected.shape, f32),
        ),
        in_specs=[SMEM, SMEM] + [VMEM] * 5 + [HBM],
        out_specs=(HBM, HBM),
        input_output_aliases={7: 1},
        scratch_shapes=[
            pltpu.VMEM((sum(part.shape[0] for part in parts), fields, lanes), bf16),
            pltpu.VMEM((span // lanes, fields, lanes), f32),
            pltpu.VMEM((tracers, 8, span), f32),
            pltpu.VMEM((fields, span), f32),
            pltpu.SemaphoreType.DMA,
            pltpu.SemaphoreType.DMA,
        ],
        compiler_params=params(16 * 1024 * 1024),
        name="rows_to_columns",
    )(slot, patch, *parts, weights, advected)


def per_device(
    tracers,
    courant,
    air_surface,
    block_weights,
    block_dest,
    block_row,
    block_patch,
    ocean_state,
    exchange_rate,
    sea_mask,
):
    tiles, subs = lax.axis_size("tile"), lax.axis_size("sub")
    devices = tiles * subs
    ocean_rows = ocean_state.shape[1]
    flat = ("tile", "sub")
    tracers_t = jnp.transpose(tracers, (1, 0, 2))
    pack_a, pack_b = pack(tracers_t, courant)
    msg_b = pass_on(lax.ppermute(
        pack_b, flat, [(i, (i + 1 if i % 2 else i - 1) % devices) for i in range(devices)]
    ))
    msg_a = lax.ppermute(pack_a, flat, [(i, i ^ 1) for i in range(devices)])

    slot, slot_back, weights = prepare(
        block_dest, block_row, block_weights, ocean_rows
    )
    state = jnp.transpose(ocean_state, (1, 0, 2))
    send, keep = forward(
        slot, block_patch, tracers[0], courant, air_surface, msg_a, msg_b, state,
        weights, devices * ocean_rows,
    )
    swap = [(0, 1), (1, 0)]
    got = lax.ppermute(send, "sub", swap)
    own, beside, *partial = merge(keep, got, state, ocean_rows)
    across = lambda x, d: lax.ppermute(x, "tile", [(i, i ^ d) for i in range(tiles)])
    got = [across(x, d) for d, x in enumerate(partial, 1)]

    advance = functools.partial(advect_some, tracers_t, courant, msg_a, msg_b)
    count = tracers.shape[1] // 3
    some, flag = advance(0, count, own)
    next_ocean, half = ocean(
        state, beside, exchange_rate, sea_mask, own, got, flag
    )

    far = [d for d in range(tiles // 2, tiles) if d % 2 == 0]
    near = list(range(1, tiles // 2))
    arrived = {d: across(half, d) for d in far[::-1] + near[::-1]}
    some, flag = advance(count, count, half, some)
    even = gather_rows([arrived[d] for d in far], flag)
    odd = across(even, 1)
    mine = gather_rows([half] + [arrived[d] for d in near] + [even])
    other = lax.ppermute(mine, "sub", swap)
    advected, flag = advance(2 * count, tracers.shape[1] - 2 * count, even, some)
    odd = gather_rows([odd], flag)
    other_odd = lax.ppermute(odd, "sub", swap)
    air_exchange, out_t = backward(
        slot_back, block_patch, (mine, odd, other, other_odd), weights, advected
    )
    return jnp.transpose(out_t, (1, 0, 2)), jnp.transpose(next_ocean, (1, 0, 2)), air_exchange


def solution(mesh):
    placed = (
        P("members", None, ("tile", "sub")),
        P("members", ("tile", "sub")),
        P("members", ("tile", "sub")),
        P(("tile", "sub"), None, None),
        P(),
        P(),
        P(("tile", "sub")),
        P("members", "sub", "tile"),
        P("sub", "tile"),
        P("sub", "tile"),
    )
    return jax.shard_map(
        per_device,
        mesh=mesh,
        in_specs=placed,
        out_specs=(
            P("members", None, ("tile", "sub")),
            P("members", "sub", "tile"),
            P("members", ("tile", "sub")),
        ),
        check_vma=False,
    )
```

```python
import functools

import jax
import jax.numpy as jnp
from jax import lax
from jax.experimental import pallas as pl
from jax.experimental.pallas import tpu as pltpu
from jax.sharding import PartitionSpec as P

ASTEPS = 3
NU = 0.2
COUPLE = 0.5
LANES = 128
EDGE = 16
GROUPS = LANES // EDGE
FORWARD_UNROLL = 256
UNROLL = 128
GROUP = 4
SETS = 2

VMEM = pl.BlockSpec(memory_space=pltpu.VMEM)
SMEM = pl.BlockSpec(memory_space=pltpu.SMEM)
ANY = pl.BlockSpec(memory_space=pl.ANY)
HBM = pl.BlockSpec(memory_space=pltpu.HBM)
f32 = jnp.float32
bf16 = jnp.bfloat16


def params(limit):
    return pltpu.CompilerParams(vmem_limit_bytes=limit)


def place():
    sizes = lax.axis_size("tile"), lax.axis_size("sub")
    return lax.axis_index("tile"), lax.axis_index("sub"), *sizes


def pass_kernel(x_ref, out_ref):
    out_ref[...] = x_ref[...]


def pass_on(x):
    return pl.pallas_call(
        pass_kernel,
        out_shape=jax.ShapeDtypeStruct(x.shape, x.dtype),
        in_specs=[VMEM],
        out_specs=VMEM,
        compiler_params=params(2 * 1024 * 1024),
        name="pass_on",
    )(x)


def is_even():
    tile, sub, _, subs = place()
    return (tile * subs + sub) % 2 == 0


def lane_roll(x, shift):
    length = x.shape[-1]
    shift = shift % length
    return x if shift == 0 else pltpu.roll(x, shift, x.ndim - 1)


def coefficients(c):
    d = 1.0 - c
    return c * d * d * (1.0 / 12.0), c * c * d * (1.0 / 12.0), c * c * (3.0 - 2.0 * c)


def advect(q, right, left, own):
    for _ in range(ASTEPS):
        pair = q + lane_roll(q, -1)
        edge = 8.0 * pair - (lane_roll(pair, 1) + lane_roll(pair, -1))
        flux = right * edge - left * lane_roll(edge, 1) + own * q
        q = q - (flux - lane_roll(flux, 1))
    return q


def pack_kernel(
    tracers, levels, q_hbm, c_hbm, a_ref, b_ref, left_t, right_t, left_c, right_c, sems
):
    span = q_hbm.shape[2]
    copies = [
        pltpu.make_async_copy(src, dst, sems.at[i])
        for i, (src, dst) in enumerate(
            (
                (q_hbm.at[:, :, pl.ds(0, LANES)], left_t),
                (q_hbm.at[:, :, pl.ds(span - LANES, LANES)], right_t),
                (c_hbm.at[:, pl.ds(0, LANES)], left_c),
                (c_hbm.at[:, pl.ds(span - LANES, LANES)], right_c),
            )
        )
    ]
    for copy in copies:
        copy.start()
    for copy in copies:
        copy.wait()
    even = is_even()
    lane = lax.broadcasted_iota(jnp.int32, (levels, LANES), 1)
    pad = pl.cdiv(levels, 8) * 8
    for out, from_left in ((a_ref, jnp.logical_not(even)), (b_ref, even)):
        for part in range(pl.cdiv(tracers + 1, GROUPS)):
            total = jnp.zeros((levels, LANES), f32)
            for group in range(GROUPS):
                item = part * GROUPS + group
                if item > tracers:
                    continue
                low = left_t[item] if item < tracers else left_c[...]
                high = right_t[item] if item < tracers else right_c[...]
                moved = jnp.where(
                    from_left,
                    lane_roll(low, EDGE * group),
                    lane_roll(high, EDGE * (group + 1)),
                )
                total = jnp.where(lane // EDGE == group, moved, total)
            out[part * pad : part * pad + levels, :] = total
        top = pl.cdiv(tracers + 1, GROUPS) * pad
        for item in range(tracers):
            out[top + item : top + item + 1, :] = jnp.where(
                from_left, left_t[item, 0:1, :], right_t[item, 0:1, :]
            )
        out[top + tracers : top + tracers + 1, :] = jnp.where(
            from_left, left_c[0:1, :], right_c[0:1, :]
        )


def pack(tracers_t, courant):
    tracers, levels, span = tracers_t.shape
    pad = pl.cdiv(levels, 8) * 8
    rows = pl.cdiv(tracers + 1, GROUPS) * pad + pl.cdiv(tracers + 1, 8) * 8
    message = jax.ShapeDtypeStruct((rows, LANES), f32)
    return pl.pallas_call(
        functools.partial(pack_kernel, tracers, levels),
        out_shape=(message, message),
        in_specs=[HBM, HBM],
        out_specs=(VMEM, VMEM),
        scratch_shapes=[
            pltpu.VMEM((tracers, levels, LANES), f32),
            pltpu.VMEM((tracers, levels, LANES), f32),
            pltpu.VMEM((levels, LANES), f32),
            pltpu.VMEM((levels, LANES), f32),
            pltpu.SemaphoreType.DMA((4,)),
        ],
        compiler_params=params(56 * 1024 * 1024),
        name="pack_edges",
    )(tracers_t, courant)


def prepare_kernel(chunk, dest_ref, row_ref, weights_hbm, slot_ref, back_ref, weights, sem):
    copy = pltpu.make_async_copy(weights_hbm, weights, sem)
    copy.start()
    tile, sub, tiles, subs = place()
    count = slot_ref.shape[0]
    mine = pl.ds((tile * subs + sub) * count, count)
    dest = dest_ref[mine, :]
    apart = (dest // subs) ^ tile
    core = (dest % subs + subs - sub) % subs * tiles
    row = row_ref[mine, :]
    slot_ref[...] = (core + apart) * chunk + row
    far = tiles // 2
    back = jnp.where(apart < far, apart, far + apart % 2 * (far // 2) + (apart - far) // 2)
    back_ref[...] = (core + back) * chunk + row
    copy.wait()


def prepare(dest, row, weights, chunk):
    blocks = weights.shape[0]
    whole = (dest.size // LANES, LANES)
    return pl.pallas_call(
        functools.partial(prepare_kernel, chunk),
        out_shape=(jax.ShapeDtypeStruct((blocks // LANES, LANES), jnp.int32),) * 2
        + (jax.ShapeDtypeStruct(weights.shape, weights.dtype),),
        in_specs=[VMEM, VMEM, HBM],
        out_specs=(VMEM, VMEM, VMEM),
        scratch_shapes=[pltpu.SemaphoreType.DMA],
        compiler_params=params(44 * 1024 * 1024),
        name="prepare_blocks",
    )(dest.reshape(whole), row.reshape(whole), weights)


def high_low(x):
    high = x.astype(bf16)
    return high, (x - high.astype(f32)).astype(bf16)


def forward_kernel(
    dims, slot_ref, patch_ref, level0, courant0, air, msg_a, msg_b, state, weights,
    send_ref, keep_ref, surface, total,
):
    tracers, span, top = dims
    blocks = weights.shape[0]
    even = is_even()
    a, b = msg_a[top : top + tracers + 1, :], msg_b[top : top + tracers + 1, :]
    left, right = jnp.where(even, b, a), jnp.where(even, a, b)
    q = jnp.concatenate([left[:tracers], level0[...], right[:tracers]], axis=1)
    c = jnp.concatenate([left[tracers:], courant0[0:1, :], right[tracers:]], axis=1)
    advected = advect(q, *coefficients(c))[:, LANES : LANES + span]
    fields = jnp.concatenate([advected, air[...]], axis=0).astype(bf16)
    for p in range(span // LANES):
        surface[p] = fields[:, p * LANES : (p + 1) * LANES]
    total[...] = jnp.zeros_like(total)
    zero = jnp.zeros(surface.shape[1:], bf16)
    height = zero.shape[0]

    def step(g, carry):
        base = g * FORWARD_UNROLL
        products = []
        for u in range(0, FORWARD_UNROLL, 2):
            first, second = surface[patch_ref[base + u]], surface[patch_ref[base + u + 1]]
            rows = jnp.concatenate(
                [jnp.concatenate([first, zero], 1), jnp.concatenate([zero, second], 1)], 0
            )
            pair = weights[pl.ds(base + u, 2)].reshape(2 * LANES, LANES)
            both = jnp.dot(rows, pair, preferred_element_type=f32)
            products += [both[:height], both[height:]]
        for u in range(FORWARD_UNROLL):
            total[slot_ref[(base + u) // LANES, (base + u) % LANES]] += products[u]
        return carry

    lax.fori_loop(0, blocks // FORWARD_UNROLL, step, 0)
    half = total.shape[0] // 2
    keep_ref[...] = total[:half]
    send_ref[:half] = total[half:].astype(bf16)
    _, sub, _, subs = place()
    beside = jnp.where(sub == subs - 1, state[0], state[state.shape[0] - 1])
    send_ref[half], send_ref[half + 1] = high_low(beside)


def forward(slot, patch, level0, courant, air, msg_a, msg_b, state, weights, rows):
    tracers, span = level0.shape
    levels = courant.shape[0]
    fields = tracers + air.shape[0]
    pad = pl.cdiv(levels, 8) * 8
    top = pl.cdiv(tracers + 1, GROUPS) * pad
    return pl.pallas_call(
        functools.partial(forward_kernel, (tracers, span, top)),
        out_shape=(
            jax.ShapeDtypeStruct((rows // 2 + 2, fields, LANES), bf16),
            jax.ShapeDtypeStruct((rows // 2, fields, LANES), f32),
        ),
        in_specs=[SMEM] * 2 + [VMEM] * 7,
        out_specs=(VMEM, VMEM),
        scratch_shapes=[
            pltpu.VMEM((span // LANES, fields, LANES), bf16),
            pltpu.VMEM((rows, fields, LANES), f32),
        ],
        compiler_params=params(28 * 1024 * 1024),
        name="blocks_to_rows",
    )(slot, patch, level0, courant, air, msg_a, msg_b, state, weights)


def with_edges(d):
    return d & (d + 1) == 0


def merge_kernel(chunk, keep, got, state, own_ref, beside_ref, *outs):
    rows, fields, lanes = state.shape
    lane = lax.broadcasted_iota(jnp.int32, (fields, lanes), 1)
    edges = jnp.zeros((fields, lanes), f32)
    for r in range(rows):
        edges = jnp.where(lane == r, lane_roll(state[r], r + 1), edges)
        edges = jnp.where(lane == rows + r, lane_roll(state[r], rows + r), edges)
    sign = jnp.where(lax.broadcasted_iota(jnp.int32, (fields, lanes), 0) < fields - 2, 1.0, -1.0)
    mirror = lax.broadcasted_iota(jnp.int32, (lanes, lanes), 0) + lax.broadcasted_iota(
        jnp.int32, (lanes, lanes), 1
    )
    mirror = jnp.where(mirror == lanes - 1, 1.0, 0.0).astype(bf16)
    fold = [
        (jnp.dot(part, mirror, preferred_element_type=f32) * sign).astype(bf16)
        for part in high_low(state[rows - 1])
    ]
    more = [*high_low(edges), *fold]
    own_ref[...] = keep[:chunk] + got[:chunk].astype(f32)
    for d, out in enumerate(outs, 1):
        part = slice(d * chunk, (d + 1) * chunk)
        out[:chunk] = (keep[part] + got[part].astype(f32)).astype(bf16)
        if with_edges(d):
            for i, extra in enumerate(more):
                out[chunk + i] = extra
    last = keep.shape[0]
    beside_ref[...] = got[last].astype(f32) + got[last + 1].astype(f32)


def merge(keep, got, state, chunk):
    rows, fields, lanes = keep.shape
    count = rows // chunk
    return pl.pallas_call(
        functools.partial(merge_kernel, chunk),
        out_shape=(
            jax.ShapeDtypeStruct((chunk, fields, lanes), f32),
            jax.ShapeDtypeStruct((fields, lanes), f32),
        )
        + tuple(
            jax.ShapeDtypeStruct((chunk + 4 * with_edges(d), fields, lanes), bf16)
            for d in range(1, count)
        ),
        in_specs=[VMEM] * 3,
        out_specs=(VMEM,) * (count + 1),
        compiler_params=params((10 if count < 16 else 24) * 1024 * 1024),
        name="merge_cores",
    )(keep, got, state)


def ocean_kernel(count, state, beside, rate, wet, own, *rest):
    got, (next_ref, half_ref) = rest[:count], rest[-2:]
    rows, fields, lanes = state.shape
    lane = lax.broadcasted_iota(jnp.int32, (fields, lanes), 1)
    tile, sub, tiles, subs = place()
    to_east, to_west = tile ^ ((tile + 1) % tiles), tile ^ ((tile + tiles - 1) % tiles)

    def extra(chunk, i):
        return chunk[rows + i].astype(f32) + chunk[rows + i + 1].astype(f32)

    from_east = from_west = jnp.zeros((fields, lanes), f32)
    for d, chunk in enumerate(got, 1):
        if with_edges(d):
            edges = extra(chunk, 0)
            from_east = jnp.where(to_east == d, edges, from_east)
            from_west = jnp.where(to_west == d, edges, from_west)
    south = jnp.where(sub == 0, 0.0, beside[...])
    north = jnp.where(sub == subs - 1, extra(got[-1], 2), beside[...])
    for r in range(rows):
        here = state[r]
        west = jnp.where(lane == 0, lane_roll(from_west, -r), lane_roll(here, 1))
        east = jnp.where(
            lane == lanes - 1, lane_roll(from_east, lanes - 1 - rows - r), lane_roll(here, -1)
        )
        below = state[r - 1] if r else south
        above = state[r + 1] if r < rows - 1 else north
        lateral = west + east + below + above - 4.0 * here
        remapped = own[r]
        for chunk in got:
            remapped = remapped + chunk[r].astype(f32)
        new = here + wet[r : r + 1, :].astype(f32) * (
            rate[r : r + 1, :] * (remapped - here) + NU * lateral
        )
        next_ref[r] = new
        half_ref[r] = new.astype(bf16)


def ocean(state, beside, rate, wet, own, got, after):
    rows, fields, lanes = state.shape
    return pl.pallas_call(
        functools.partial(ocean_kernel, len(got)),
        out_shape=(
            jax.ShapeDtypeStruct(state.shape, f32),
            jax.ShapeDtypeStruct(state.shape, bf16),
        ),
        in_specs=[VMEM] * (5 + len(got)) + [ANY],
        out_specs=(VMEM, VMEM),
        compiler_params=params(8 * 1024 * 1024),
        name="ocean_update",
    )(state, beside, rate, wet, own, *got, after)


def gather_kernel(count, *refs):
    out, start = refs[-1], 0
    for ref in refs[:count]:
        out[start : start + ref.shape[0]] = ref[...]
        start += ref.shape[0]


def gather_rows(parts, *after):
    fields, lanes = parts[0].shape[1:]
    rows = sum(part.shape[0] for part in parts)
    return pl.pallas_call(
        functools.partial(gather_kernel, len(parts)),
        out_shape=jax.ShapeDtypeStruct((rows, fields, lanes), bf16),
        in_specs=[VMEM] * len(parts) + [ANY] * len(after),
        out_specs=VMEM,
        compiler_params=params(8 * 1024 * 1024),
        name="gather_rows",
    )(*parts, *after)


def advect_kernel(
    tracers, levels, first, group, q_ref, c_ref, msg_a, msg_b, *rest
):
    out_ref, flag_ref, right, left, own, band, *scratch = rest[-6 - 2 * SETS :]
    even = is_even()
    span = q_ref.shape[2]
    pad = pl.cdiv(levels, 8) * 8
    tiles = span // LANES + 2
    tile = lambda i: slice(i * LANES, (i + 1) * LANES)

    def sides(item):
        start = pl.multiple_of(item // GROUPS * pad, 8)
        shift = EDGE * (item % GROUPS)
        a, b = msg_a[pl.ds(start, levels), :], msg_b[pl.ds(start, levels), :]
        before, after = jnp.where(even, b, a), jnp.where(even, a, b)
        return (
            pltpu.roll(before, (2 * LANES - EDGE - shift) % LANES, 1),
            pltpu.roll(after, (LANES - shift) % LANES, 1),
        )

    @pl.when(pl.program_id(0) == 0)
    def _():
        before, after = sides(tracers)
        c = jnp.concatenate([before, c_ref[...], after], axis=1)
        for ref, value in zip((right, left, own), coefficients(c)):
            ref[...] = jnp.zeros_like(ref)
            for i in range(tiles):
                ref[i, :levels] = value[:, tile(i)]
        for state in scratch[:SETS]:
            state[...] = jnp.zeros_like(state)
        r = lax.broadcasted_iota(jnp.int32, band.shape, 0) % (2 * LANES)
        j = lax.broadcasted_iota(jnp.int32, band.shape, 1)
        column = jnp.where(r < LANES, r, jnp.where(r < LANES + LANES // 2, r, r - 2 * LANES))
        d = column - jnp.where(j < LANES, j, j - LANES - 1)
        weight = jnp.where((d == 0) | (d == 1), 7.0, jnp.where((d == -1) | (d == 2), -1.0, 0.0))
        band[...] = weight.astype(bf16)
        flag_ref[...] = jnp.zeros_like(flag_ref)

    sets = SETS
    states, operands = scratch[:sets], scratch[sets:]
    each = group // sets
    for t in range(group):
        state, at = states[t // each], t % each
        before, after = sides(pl.program_id(0) * group + first + t)
        part = slice(at * pad, at * pad + levels)
        state[0, part] = before
        for i in range(1, tiles - 1):
            state[i, part] = q_ref[t, :, tile(i - 1)]
        state[tiles - 1, part] = after

    rows = each * pad
    lane = lax.broadcasted_iota(jnp.int32, (rows, LANES), 1)

    def edge_values(state, lhs):
        halves = [high_low(state[i]) for i in range(tiles)]
        for i in range(tiles):
            part = slice(i * rows, (i + 1) * rows)
            for h in range(2):
                lhs[part, tile(2 * h)] = halves[i][h]
                lhs[part, tile(2 * h + 1)] = jnp.where(
                    lane < LANES // 2, halves[min(i + 1, tiles - 1)][h], halves[max(i - 1, 0)][h]
                )
        return jnp.dot(lhs[...], band[...], preferred_element_type=f32)

    def advance(state, edges):
        last = None
        for i in range(tiles):
            edge = edges[i * rows : (i + 1) * rows].reshape(each, pad, 2 * LANES)
            q = state[i]
            flux = (
                right[i] * edge[..., :LANES]
                - left[i] * edge[..., LANES:]
                + own[i] * q.reshape(each, pad, LANES)
            ).reshape(rows, LANES)
            moved = pltpu.roll(flux, 1, 1)
            before = moved if last is None else jnp.where(lane == 0, last, moved)
            state[i] = q - (flux - before)
            last = moved

    pending = None
    for step in range(ASTEPS):
        for k in range(sets):
            edges = edge_values(states[k], operands[k])
            if pending is not None:
                advance(*pending)
            pending = (states[k], edges)
    advance(*pending)

    for t in range(group):
        for i in range(1, tiles - 1):
            at = t % each * pad
            out_ref[t, :, tile(i - 1)] = states[t // each][i, at : at + levels]


def advect_some(tracers_t, courant, msg_a, msg_b, first, count, after, into=None):
    tracers, levels, span = tracers_t.shape
    group = GROUP
    tiles, pad = span // LANES + 2, pl.cdiv(levels, 8) * 8
    whole = lambda shape: pl.BlockSpec(shape, lambda i: (0,) * len(shape))
    block = pl.BlockSpec((group, levels, span), lambda i: (i + first // group, 0, 0))
    more = [after] if into is None else [after, into]
    return pl.pallas_call(
        functools.partial(advect_kernel, tracers, levels, first, group),
        grid=(count // group,),
        out_shape=(
            jax.ShapeDtypeStruct(tracers_t.shape, f32),
            jax.ShapeDtypeStruct((8, LANES), f32),
        ),
        in_specs=[
            block,
            whole(courant.shape),
            whole(msg_a.shape),
            whole(msg_b.shape),
        ]
        + [ANY] * len(more),
        out_specs=(block, whole((8, LANES))),
        input_output_aliases={} if into is None else {5: 0},
        scratch_shapes=[pltpu.VMEM((tiles, pad, LANES), f32)] * 3
        + [pltpu.VMEM((4 * LANES, 2 * LANES), bf16)]
        + [pltpu.VMEM((tiles, group // SETS * pad, LANES), f32)] * SETS
        + [pltpu.VMEM((tiles * group // SETS * pad, 4 * LANES), bf16)] * SETS,
        compiler_params=params(12 * 1024 * 1024),
        cost_estimate=pl.CostEstimate(
            flops=200 * count * levels * span,
            bytes_accessed=8 * count * levels * span,
            transcendentals=0,
        ),
        name="advect_levels",
    )(tracers_t, courant, msg_a, msg_b, *more)


def backward_kernel(
    slot_ref, patch_ref, mine, odd, other, other_odd, weights, advected_hbm, air_hbm, out_hbm,
    rows, total, bottom, air, sem, air_sem,
):
    fetch = pltpu.make_async_copy(advected_hbm.at[:, pl.ds(0, 1), :], bottom, sem)
    fetch.start()
    tracers, _, span = bottom.shape
    blocks = weights.shape[0]
    fields = mine.shape[1]
    start = 0
    for some in (mine, odd, other, other_odd):
        rows[start : start + some.shape[0]] = some[...]
        start += some.shape[0]
    total[...] = jnp.zeros_like(total)
    slot_of = lambda b: slot_ref[b // LANES, b % LANES]

    def step(g, carry):
        base = g * UNROLL
        products = []
        for u in range(0, UNROLL, 2):
            both = lax.dot_general(
                jnp.concatenate([rows[slot_of(base + u)], rows[slot_of(base + u + 1)]], 0),
                weights[pl.ds(base + u, 2)].reshape(2 * LANES, LANES),
                (((1,), (1,)), ((), ())),
                preferred_element_type=f32,
            )
            products += [both[:fields, :LANES], both[fields:, LANES:]]
        for u in range(UNROLL):
            total[patch_ref[base + u]] += products[u]
        return carry

    lax.fori_loop(0, blocks // UNROLL, step, 0)
    fetch.wait()
    for p in range(span // LANES):
        part = slice(p * LANES, (p + 1) * LANES)
        exchange = total[p]
        air[:, part] = exchange
        bottom[:, 0, part] += COUPLE * exchange[:tracers]
    stores = (
        pltpu.make_async_copy(bottom, out_hbm.at[:, pl.ds(0, 1), :], sem),
        pltpu.make_async_copy(air, air_hbm, air_sem),
    )
    for store in stores:
        store.start()
    for store in stores:
        store.wait()


def backward(slot, patch, parts, weights, advected):
    tracers, levels, span = advected.shape
    fields, lanes = parts[0].shape[1:]
    return pl.pallas_call(
        backward_kernel,
        out_shape=(
            jax.ShapeDtypeStruct((fields, span), f32),
            jax.ShapeDtypeStruct(advected.shape, f32),
        ),
        in_specs=[SMEM, SMEM] + [VMEM] * 5 + [HBM],
        out_specs=(HBM, HBM),
        input_output_aliases={7: 1},
        scratch_shapes=[
            pltpu.VMEM((sum(part.shape[0] for part in parts), fields, lanes), bf16),
            pltpu.VMEM((span // lanes, fields, lanes), f32),
            pltpu.VMEM((tracers, 1, span), f32),
            pltpu.VMEM((fields, span), f32),
            pltpu.SemaphoreType.DMA,
            pltpu.SemaphoreType.DMA,
        ],
        compiler_params=params(16 * 1024 * 1024),
        name="rows_to_columns",
    )(slot, patch, *parts, weights, advected)


def per_device(
    tracers,
    courant,
    air_surface,
    block_weights,
    block_dest,
    block_row,
    block_patch,
    ocean_state,
    exchange_rate,
    sea_mask,
):
    tiles, subs = lax.axis_size("tile"), lax.axis_size("sub")
    devices = tiles * subs
    ocean_rows = ocean_state.shape[1]
    flat = ("tile", "sub")
    tracers_t = jnp.transpose(tracers, (1, 0, 2))
    pack_a, pack_b = pack(tracers_t, courant)
    msg_b = pass_on(lax.ppermute(
        pack_b, flat, [(i, (i + 1 if i % 2 else i - 1) % devices) for i in range(devices)]
    ))
    msg_a = lax.ppermute(pack_a, flat, [(i, i ^ 1) for i in range(devices)])

    slot, slot_back, weights = prepare(
        block_dest, block_row, block_weights, ocean_rows
    )
    state = jnp.transpose(ocean_state, (1, 0, 2))
    send, keep = forward(
        slot, block_patch, tracers[0], courant, air_surface, msg_a, msg_b, state,
        weights, devices * ocean_rows,
    )
    swap = [(0, 1), (1, 0)]
    got = lax.ppermute(send, "sub", swap)
    own, beside, *partial = merge(keep, got, state, ocean_rows)
    across = lambda x, d: lax.ppermute(x, "tile", [(i, i ^ d) for i in range(tiles)])
    got = [across(x, d) for d, x in enumerate(partial, 1)]

    advance = functools.partial(advect_some, tracers_t, courant, msg_a, msg_b)
    count = tracers.shape[1] // 3
    some, flag = advance(0, count, own)
    next_ocean, half = ocean(
        state, beside, exchange_rate, sea_mask, own, got, flag
    )

    far = [d for d in range(tiles // 2, tiles) if d % 2 == 0]
    near = list(range(1, tiles // 2))
    arrived = {d: across(half, d) for d in far[::-1] + near[::-1]}
    some, flag = advance(count, count, half, some)
    even = gather_rows([arrived[d] for d in far], flag)
    odd = across(even, 1)
    mine = gather_rows([half] + [arrived[d] for d in near] + [even])
    other = lax.ppermute(mine, "sub", swap)
    advected, flag = advance(2 * count, tracers.shape[1] - 2 * count, even, some)
    odd = gather_rows([odd], flag)
    other_odd = lax.ppermute(odd, "sub", swap)
    air_exchange, out_t = backward(
        slot_back, block_patch, (mine, odd, other, other_odd), weights, advected
    )
    return jnp.transpose(out_t, (1, 0, 2)), jnp.transpose(next_ocean, (1, 0, 2)), air_exchange


def solution(mesh):
    placed = (
        P("members", None, ("tile", "sub")),
        P("members", ("tile", "sub")),
        P("members", ("tile", "sub")),
        P(("tile", "sub"), None, None),
        P(),
        P(),
        P(("tile", "sub")),
        P("members", "sub", "tile"),
        P("sub", "tile"),
        P("sub", "tile"),
    )
    return jax.shard_map(
        per_device,
        mesh=mesh,
        in_specs=placed,
        out_specs=(
            P("members", None, ("tile", "sub")),
            P("members", "sub", "tile"),
            P("members", ("tile", "sub")),
        ),
        check_vma=False,
    )
```
